32 devices in a mesh: sta: 8 (over y, x, core), cel: 4 (over z).
Axes of the slice: x: 2, y: 2, z: 4, core: 2. Of those that a mesh axis runs over, the one named last changes fastest.
Arguments:
- station_plane: int32 [2, 32768], P(None, 'sta'), may hold values from 0 to 191
- station_height: int32 [32768], P('sta'), may hold values from 1 to 4
- cell_plane: int32 [2, 8192], P(None, 'cel'), may hold values from 0 to 191
- cell_depth: int32 [8192], P('cel'), may hold values from 0 to 15
- cell_density: float32 [8192], P('cel'), may hold values from 0.4 to 4
- left_before: float32 [16, 32768], P(None, 'sta'), may hold values from -6 to 6
- left_now: float32 [16, 32768], P(None, 'sta'), may hold values from -6 to 6
- right_before: float32 [16, 8192], P(None, 'cel'), may hold values from -6 to 6
Outputs:
- right_blocks: float32 [2, 16, 8192], P(None, None, 'cel')
- left_block: float32 [16, 32768], P(None, 'sta')
- alphas: float32 [2, 16, 16], replicated
- betas: float32 [2, 16, 16], replicated
The draws below stay inside these ranges and needn't reach their ends.
All inputs are finite; a program needn't handle non-finite values.
Results may differ from the reference program's by a relative error of at most 0.0003.
Values sent between devices are 32-bit elements; how exact they have to be, the bound alone decides.
A program may use at most 64 MiB of HBM per device.

```python
import math
import jax
import jax.numpy as jnp
from jax import lax

RHS = 16
STEPS = 2
SPAN = 192
DEPTH = 16
STATIONS = 32768
CELLS = 8192


def set_ends(result, stream_key, least, top_value):
    longest = result.shape.index(max(result.shape))
    spots = []
    for shift in (0, 1):
        where = [jax.random.randint(jax.random.fold_in(stream_key, axis), (), 0, length) for axis, length in enumerate(result.shape)]
        where[longest] = (where[longest] + shift) % result.shape[longest]
        spots.append(tuple(where))
    return result.at[spots[0]].set(least).at[spots[1]].set(top_value)


def block_scale(rng, extent, cuts, smallest, largest):
    gain, own = 1.0, jax.random.fold_in(rng, 6)
    for position, blocks in cuts:
        heights = jnp.exp(jax.random.uniform(jax.random.fold_in(own, position), (blocks,), jnp.float32, smallest / len(cuts), largest / len(cuts)))
        gain = gain * jnp.repeat(heights, extent[position] // blocks).reshape([-1 if axis == position else 1 for axis in range(len(extent))])
    return gain


def scatter_about(rng, shape, spread, most, shards=(), dtype=jnp.bfloat16):
    array = jax.random.normal(rng, shape, jnp.float32) * spread
    if len(shards) > 0:
        array = block_scale(rng, shape, shards, -0.22, 0.18) * array
    return jnp.clip(array, min=-most, max=most).astype(dtype)


def setup_inputs(seed: int = 0) -> dict:
    key_list = jax.random.split(jax.random.key(seed), 9)
    station_plane = set_ends(jax.random.randint(key_list[0], (2, STATIONS), 0, SPAN), jax.random.fold_in(key_list[0], 1), 0, SPAN - 1).astype(jnp.int32)
    station_height = set_ends(jax.random.randint(key_list[1], (STATIONS,), 1, 5), jax.random.fold_in(key_list[1], 1), 1, 4).astype(jnp.int32)
    cell_plane = set_ends(jax.random.randint(key_list[2], (2, CELLS), 0, SPAN), jax.random.fold_in(key_list[2], 1), 0, SPAN - 1).astype(jnp.int32)
    cell_depth = set_ends(jax.random.randint(key_list[3], (CELLS,), 0, DEPTH), jax.random.fold_in(key_list[3], 1), 0, DEPTH - 1).astype(jnp.int32)
    cell_density = jnp.clip(jnp.exp(math.log(4.0) - 2.3025851 * jax.random.uniform(key_list[4], (CELLS,), jnp.float32) ** block_scale(key_list[4], (CELLS,), ((0, 4),), -0.2, 0.2)), 0.4, 4.0)
    left_before = scatter_about(key_list[5], (RHS, STATIONS), 1.0, 6.0, ((1, 8),), jnp.float32)
    left_now = scatter_about(key_list[6], (RHS, STATIONS), 1.0, 6.0, ((1, 8),), jnp.float32)
    right_before = scatter_about(key_list[7], (RHS, CELLS), 1.0, 6.0, ((1, 4),), jnp.float32)
    return {"station_plane": station_plane, "station_height": station_height, "cell_plane": cell_plane, "cell_depth": cell_depth, "cell_density": cell_density, "left_before": left_before, "left_now": left_now, "right_before": right_before}


GAIN = 4.0
HIGH = lax.Precision.HIGHEST

def kernel_rows(sx, sy, sz, cx, cy, cz, density):
    dx = sx[:, None] - cx[None, :]
    dy = sy[:, None] - cy[None, :]
    dz = sz[:, None] + cz[None, :] + 0.5
    square = dx * dx + dy * dy + dz * dz
    inverse = lax.rsqrt(square)
    inv_two = inverse * inverse
    return GAIN * density[None, :] * (2.0 * dz * dz - dx * dx - dy * dy) * (inv_two * inv_two * inverse)

def matmul(a, b):
    return jnp.dot(a.astype(jnp.float32), b.astype(jnp.float32), precision=HIGH, preferred_element_type=jnp.float32)

def orthonormal(block, basis, rows):
    coef = matmul(basis, block.T) / rows
    rest = block - matmul(coef.T, basis)
    gram = matmul(rest, rest.T) / rows
    lower = jnp.linalg.cholesky(gram)
    return (jax.scipy.linalg.solve_triangular(lower, rest, lower=True), lower)

def reference(station_plane, station_height, cell_plane, cell_depth, cell_density, left_before, left_now, right_before):
    sx = station_plane[0].astype(jnp.float32)
    sy = station_plane[1].astype(jnp.float32)
    sz = station_height.astype(jnp.float32)
    cx = cell_plane[0].astype(jnp.float32)
    cy = cell_plane[1].astype(jnp.float32)
    cz = cell_depth.astype(jnp.float32)
    block = 1024 if STATIONS % 1024 == 0 else STATIONS
    count = STATIONS // block
    sx_b = sx.reshape(count, block)
    sy_b = sy.reshape(count, block)
    sz_b = sz.reshape(count, block)

    def adjoint(left):
        left_b = left.reshape(RHS, count, block).transpose(1, 0, 2)

        def add_block(total, pieces):
            a, b, c, rows = pieces
            return (total + matmul(rows, kernel_rows(a, b, c, cx, cy, cz, cell_density)), None)
        total, unused = lax.scan(add_block, jnp.zeros((RHS, CELLS), jnp.float32), (sx_b, sy_b, sz_b, left_b))
        return total

    def forward(right):

        def one_block(pieces):
            a, b, c = pieces
            return matmul(right, kernel_rows(a, b, c, cx, cy, cz, cell_density).T)
        parts = lax.map(one_block, (sx_b, sy_b, sz_b))
        return parts.transpose(1, 0, 2).reshape(RHS, STATIONS)
    right_basis = right_before
    left_basis = jnp.concatenate([left_before, left_now], 0)
    left = left_now
    rights, alphas, betas = ([], [], [])
    for step in range(STEPS):
        right, alpha = orthonormal(adjoint(left), right_basis, CELLS)
        right_basis = jnp.concatenate([right_basis, right], 0)
        left, beta = orthonormal(forward(right), left_basis, STATIONS)
        left_basis = jnp.concatenate([left_basis, left], 0)
        rights.append(right)
        alphas.append(alpha)
        betas.append(beta)
    return (jnp.stack(rights), left, jnp.stack(alphas), jnp.stack(betas))
```

```python
import functools

import jax
import jax.numpy as jnp
from jax import lax
from jax.experimental import pallas as pl
from jax.experimental.pallas import tpu as pltpu
from jax.sharding import PartitionSpec as P

STEPS = 2
GAIN = 4.0
CENTER = 96.0
FEATURES = 16
HIGH = lax.Precision.HIGHEST
F32 = jnp.float32
BF16 = jnp.bfloat16
MESH = pl.DeviceIdType.MESH
NN = (((1,), (0,)), ((), ()))
NT = (((1,), (1,)), ((), ()))
TN = (((0,), (0,)), ((), ()))


def dot(a, b, dims, precision=None):
    return lax.dot_general(a, b, dims, precision=precision, preferred_element_type=F32)


def split(values):
    high = values.astype(BF16)
    return high, (values - high.astype(F32)).astype(BF16)


def station_features(plane, height):
    x = plane[0].astype(F32) - CENTER
    y = plane[1].astype(F32) - CENTER
    z = height.astype(F32)
    flat = x * x + y * y
    high = jnp.floor(flat / 256.0) * 256.0
    one = jnp.ones_like(x)
    zero = jnp.zeros_like(x)
    rows = [high, flat - high, one, one, x, y, z * z, z, one, one]
    rows += [zero] * (FEATURES - len(rows))
    return jnp.stack(rows).astype(BF16)


def cell_features(plane, depth):
    x = plane[0].astype(F32) - CENTER
    y = plane[1].astype(F32) - CENTER
    z = depth.astype(F32)
    flat = x * x + y * y
    high = jnp.floor(flat / 256.0) * 256.0
    low = flat - high
    one = jnp.ones_like(x)
    zero = jnp.zeros_like(x)
    pad = [zero] * (FEATURES - 10)
    square = [one, one, high, low, -2.0 * x, -2.0 * y, one, 2.0 * z + one, z * z + z, 0.25 * one]
    top = [-one, -one, -high, -low, 2.0 * x, 2.0 * y, 2.0 * one, 4.0 * z + 2.0 * one]
    top += [2.0 * (z * z + z), 0.5 * one]
    return jnp.stack(square + pad).astype(BF16), jnp.stack(top + pad).astype(BF16)


def eliminate(gram):
    width = gram.shape[0]
    row = lax.broadcasted_iota(jnp.int32, (width, width), 0)
    col = lax.broadcasted_iota(jnp.int32, (width, width), 1)
    eye = (row == col).astype(F32)
    upper, inverse = gram, eye
    for j in range(width - 1):
        pivot = upper[j : j + 1, :]
        factor = jnp.where(row[:, :1] > j, upper[:, j : j + 1] / pivot[:, j : j + 1], 0.0)
        upper = upper - factor * pivot
        inverse = inverse - factor * inverse[j : j + 1, :]
    scale = lax.rsqrt(jnp.sum(eye * upper, axis=1, keepdims=True))
    upper = jnp.where(col >= row, upper * scale, 0.0)
    lower = dot(upper, eye, TN, HIGH)
    return inverse * scale, lower


def combination(sums, basis_gram, rows):
    width = sums.shape[0]
    scaled = sums / rows
    square, coef = scaled[:, :width], scaled[:, width:]
    gram = square - 2.0 * dot(coef, coef, NT, HIGH)
    gram = gram + dot(dot(coef, basis_gram / rows, NN, HIGH), coef, NT, HIGH)
    inverse, lower = eliminate(gram)
    return inverse, coef, lower


def kernel(
    n_sta, n_cel, fs, c_square, c_top, density, before, now, right_before,
    rights, left, alphas, betas,
    g_high, g_low, lhs, gp, forward, rhs, w_full, v_full, z_right, z_left, station_buf, cell_buf,
    small_right, small_left, part,
    sta_send, sta_recv, cel_send, cel_recv, sr_send, sr_recv, sl_send, sl_recv,
):
    width, s_dev = now.shape
    c_dev = right_before.shape[1]
    s_me = lax.axis_index("sta")
    c_me = lax.axis_index("cel")
    cells = float(c_dev * n_cel)
    stations = float(s_dev * n_sta)

    def group(axis):
        me, n = (s_me, n_sta) if axis == "sta" else (c_me, n_cel)
        return [(o, lax.rem(me + o, n)) for o in range(1, n)]

    barrier = pltpu.get_barrier_semaphore()
    for axis in ("sta", "cel"):
        for _, peer in group(axis):
            pl.semaphore_signal(barrier, inc=1, device_id={axis: peer}, device_id_type=MESH)

    def broadcast(axis, source, target, send, recv):
        copies = []
        for o, peer in group(axis):
            copies.append(pltpu.make_async_remote_copy(
                src_ref=source(peer), dst_ref=target, send_sem=send.at[o], recv_sem=recv.at[o],
                device_id={axis: peer}, device_id_type=MESH))
            copies[-1].start()
        return copies

    def finish(copies):
        for copy in copies:
            copy.wait()

    def all_reduce(axis, step, full, buf, send, recv):
        me, n = (s_me, n_sta) if axis == "sta" else (c_me, n_cel)
        share = full.shape[2] // n

        def columns(index):
            return pl.ds(pl.multiple_of(index * share, 128), share)

        mine = columns(me)
        copies = broadcast(
            axis, lambda peer: part.at[:, columns(peer)] if axis == "cel" else gp.at[0, :, columns(peer)],
            buf.at[step, me], send.at[step, 0], recv.at[step, 0])
        own = part[:, mine] if axis == "cel" else gp[0, :, mine]
        finish(copies)
        total = own
        for o, peer in group(axis):
            total = total + buf[step, peer]
        if axis == "sta":
            total = total * density[:, mine]
        full[step, :, mine] = total
        block = full.at[step, :, mine]
        finish(broadcast(axis, lambda peer: block, block, send.at[step, 1], recv.at[step, 1]))

    def small_start(axis, step, z, buf, send, recv):
        me = s_me if axis == "sta" else c_me
        rows = z.shape[0]
        buf[step, me, :rows, :rows] = dot(z, z, NT, HIGH)
        block = buf.at[step, me]
        return broadcast(axis, lambda peer: block, block, send.at[step], recv.at[step])

    def small_end(copies, step, rows, buf):
        finish(copies)
        total = buf[step, 0, :rows, :rows]
        for index in range(1, buf.shape[1]):
            total = total + buf[step, index, :rows, :rows]
        return total

    def mix(inverse, coef, block, basis):
        rest = block
        for index, piece in enumerate(basis):
            rest = rest - dot(coef[:, index * width : (index + 1) * width], piece, NN, HIGH)
        return dot(inverse, rest, NN, HIGH)

    high, low = split(now[...])
    lhs[:width], lhs[2 * width : 3 * width] = high, low
    high, low = split(before[...])
    lhs[width : 2 * width], lhs[3 * width :] = high, low
    gp[...] = jnp.zeros_like(gp)
    s_tile, c_tile = 256, 512
    across = c_dev // c_tile

    def make_tile(index, carry):
        rows = pl.ds(pl.multiple_of(index // across * s_tile, s_tile), s_tile)
        cols = pl.ds(pl.multiple_of(index % across * c_tile, c_tile), c_tile)
        feature = fs[:, rows]
        square = dot(feature, c_square[:, cols], TN)
        top = dot(feature, c_top[:, cols], TN)
        inverse = lax.rsqrt(square)
        two = inverse * inverse
        high, low = split(two * two * (top * inverse))
        g_high[rows, cols] = high
        g_low[rows, cols] = low
        first = dot(lhs[:, rows], high, NN)
        second = dot(lhs[: 2 * width, rows], low, NN)
        for b in range(2):
            gp[b, :, cols] += (
                first[b * width : (b + 1) * width]
                + first[(b + 2) * width : (b + 3) * width]
                + second[b * width : (b + 1) * width]
            )
        return carry

    lax.fori_loop(0, s_dev // s_tile * across, make_tile, 0)
    gp[2] = gp[0]
    pl.semaphore_wait(barrier, n_sta + n_cel - 2)

    left_grams = None
    for step in range(STEPS):
        all_reduce("sta", step, w_full, station_buf, sta_send, sta_recv)
        w = w_full[step]
        z_right[:width] = w
        if step == 0:
            z_right[width : 2 * width] = right_before[...]
        rows = (step + 2) * width
        copies = small_start("cel", step, z_right[:rows], small_right, sr_send, sr_recv)
        high, low = split(w * density[...])
        rhs[:width], rhs[2 * width : 3 * width] = high, low
        if step == 0:
            high, low = split(right_before[...] * density[...])
            rhs[width : 2 * width], rhs[3 * width :] = high, low
        f_tile = 512

        def forward_tile(index, carry):
            span = pl.ds(pl.multiple_of(index * f_tile, f_tile), f_tile)
            first = dot(rhs[...], g_high[span, :], NT)
            second = dot(rhs[: 2 * width], g_low[span, :], NT)
            both = first[: 2 * width] + first[2 * width :] + second
            part[:, span] = both[:width]
            if step == 0:
                forward[0, :, span] = both[width:]
            return carry

        lax.fori_loop(0, s_dev // f_tile, forward_tile, 0)
        sums = small_end(copies, step, rows, small_right)
        inverse, coef, lower = combination(sums[:width], sums[width:, width:], cells)
        alphas[step] = lower
        basis = [z_right[(b + 1) * width : (b + 2) * width] for b in range(step + 1)]
        right = mix(inverse, coef, w, basis)
        rights[step] = right
        values = mix(inverse, coef, part[...], [forward[b] for b in range(step + 1)])
        part[...] = values
        if step + 1 < STEPS:
            z_right[(step + 2) * width : (step + 3) * width] = right
            forward[step + 1] = values

        all_reduce("cel", step, v_full, cell_buf, cel_send, cel_recv)
        v = v_full[step]
        z_left[:width] = v
        if step == 0:
            z_left[width : 2 * width] = before[...]
            z_left[2 * width : 3 * width] = now[...]
        rows = (step + 3) * width
        copies = small_start("sta", step, z_left[:rows], small_left, sl_send, sl_recv)
        if step + 1 < STEPS:
            high, low = split(v)
            lhs[:width], lhs[width : 2 * width] = high, low
            b_tile = 256

            def adjoint_tile(index, carry):
                span = pl.ds(pl.multiple_of(index * b_tile, b_tile), b_tile)
                first = dot(lhs[: 2 * width], g_high[:, span], NN)
                second = dot(lhs[:width], g_low[:, span], NN)
                gp[0, :, span] = first[:width] + first[width:] + second
                return carry

            lax.fori_loop(0, c_dev // b_tile, adjoint_tile, 0)
        sums = small_end(copies, step, rows, small_left)
        inverse, coef, lower = combination(sums[:width], sums[width:, width:], stations)
        betas[step] = lower
        basis = [z_left[(b + 1) * width : (b + 2) * width] for b in range(step + 2)]
        block = mix(inverse, coef, v, basis)
        if step + 1 < STEPS:
            z_left[(step + 3) * width : (step + 4) * width] = block
            values = mix(inverse, coef, gp[0], [gp[b + 1] for b in range(step + 2)])
            gp[0] = values
            if step + 2 < STEPS:
                gp[step + 3] = values
        else:
            left[...] = block


def body(plane, height, cell_plane, depth, density, before, now, right_before):
    width, s_dev = now.shape
    c_dev = right_before.shape[1]
    n_sta = lax.axis_size("sta")
    n_cel = lax.axis_size("cel")
    fs = station_features(plane, height)
    c_square, c_top = cell_features(cell_plane, depth)
    vmem = pl.BlockSpec(memory_space=pltpu.VMEM)
    dma = pltpu.SemaphoreType.DMA
    lanes = 128
    out_shape = (
        jax.ShapeDtypeStruct((STEPS, width, c_dev), F32),
        jax.ShapeDtypeStruct((width, s_dev), F32),
        jax.ShapeDtypeStruct((STEPS, width, width), F32),
        jax.ShapeDtypeStruct((STEPS, width, width), F32),
    )
    scratch = [
        pltpu.VMEM((s_dev, c_dev), BF16),
        pltpu.VMEM((s_dev, c_dev), BF16),
        pltpu.VMEM((4 * width, s_dev), BF16),
        pltpu.VMEM((STEPS + 1, width, c_dev), F32),
        pltpu.VMEM((STEPS, width, s_dev), F32),
        pltpu.VMEM((4 * width, c_dev), BF16),
        pltpu.VMEM((STEPS, width, c_dev), F32),
        pltpu.VMEM((STEPS, width, s_dev), F32),
        pltpu.VMEM(((STEPS + 1) * width, c_dev), F32),
        pltpu.VMEM(((STEPS + 2) * width, s_dev), F32),
        pltpu.VMEM((STEPS, n_sta, width, c_dev // n_sta), F32),
        pltpu.VMEM((STEPS, n_cel, width, s_dev // n_cel), F32),
        pltpu.VMEM((STEPS, n_cel, (STEPS + 1) * width, lanes), F32),
        pltpu.VMEM((STEPS, n_sta, (STEPS + 2) * width, lanes), F32),
        pltpu.VMEM((width, s_dev), F32),
        dma((STEPS, 2, n_sta)),
        dma((STEPS, 2, n_sta)),
        dma((STEPS, 2, n_cel)),
        dma((STEPS, 2, n_cel)),
        dma((STEPS, n_cel)),
        dma((STEPS, n_cel)),
        dma((STEPS, n_sta)),
        dma((STEPS, n_sta)),
    ]
    rights, left, alphas, betas = pl.pallas_call(
        functools.partial(kernel, n_sta, n_cel),
        out_shape=out_shape,
        in_specs=[vmem] * 7,
        out_specs=(vmem,) * 4,
        scratch_shapes=scratch,
        compiler_params=pltpu.CompilerParams(
            collective_id=0, has_side_effects=True, vmem_limit_bytes=56 * 1024 * 1024
        ),
        cost_estimate=pl.CostEstimate(
            flops=2 * 3 * 2 * STEPS * width * s_dev * c_dev, bytes_accessed=4 * 1024 * 1024, transcendentals=s_dev * c_dev
        ),
    )(fs, c_square, c_top, (GAIN * density)[None, :], before, now, right_before)
    return rights, left, alphas, betas


def solution(mesh):
    in_specs = (
        P(None, "sta"),
        P("sta"),
        P(None, "cel"),
        P("cel"),
        P("cel"),
        P(None, "sta"),
        P(None, "sta"),
        P(None, "cel"),
    )
    out_specs = (P(None, None, "cel"), P(None, "sta"), P(), P())
    return jax.shard_map(body, mesh=mesh, in_specs=in_specs, out_specs=out_specs, check_vma=False)
```

```python
import functools

import jax
import jax.numpy as jnp
from jax import lax
from jax.experimental import pallas as pl
from jax.experimental.pallas import tpu as pltpu
from jax.sharding import PartitionSpec as P

STEPS = 2
GAIN = 4.0
CENTER = 96.0
FEATURES = 16
HIGH = lax.Precision.HIGHEST
F32 = jnp.float32
BF16 = jnp.bfloat16
MESH = pl.DeviceIdType.MESH
NN = (((1,), (0,)), ((), ()))
NT = (((1,), (1,)), ((), ()))
TN = (((0,), (0,)), ((), ()))


def dot(a, b, dims, precision=None):
    return lax.dot_general(a, b, dims, precision=precision, preferred_element_type=F32)


def split(values):
    high = values.astype(BF16)
    return high, (values - high.astype(F32)).astype(BF16)


def fill_features(ref, rows):
    for index, row in enumerate(rows):
        ref[index : index + 1, :] = row
    ref[len(rows) :, :] = jnp.zeros((FEATURES - len(rows), ref.shape[1]), F32)


def coordinates(plane, level):
    x = plane[0:1, :].astype(F32) - CENTER
    y = plane[1:2, :].astype(F32) - CENTER
    z = level[...].astype(F32)
    flat = x * x + y * y
    high = jnp.floor(flat / 256.0) * 256.0
    return x, y, z, high, flat - high, jnp.ones_like(x)


def station_features(ref, plane, height):
    x, y, z, high, low, one = coordinates(plane, height)
    fill_features(ref, [high, low, one, one, x, y, z * z, z, one, one])


def cell_features(square, top, plane, depth):
    x, y, z, high, low, one = coordinates(plane, depth)
    inner = z * z + z
    rows = [one, one, high, low, -2.0 * x, -2.0 * y, one, 2.0 * z + one, inner, 0.25 * one]
    fill_features(square, rows)
    rows = [-one, -one, -high, -low, 2.0 * x, 2.0 * y, 2.0 * one, 4.0 * z + 2.0 * one]
    fill_features(top, rows + [2.0 * inner, 0.5 * one])


def eliminate(gram):
    width = gram.shape[0]
    row = lax.broadcasted_iota(jnp.int32, (width, width), 0)
    col = lax.broadcasted_iota(jnp.int32, (width, width), 1)
    eye = (row == col).astype(F32)
    upper, inverse = gram, eye
    for j in range(width - 1):
        pivot = upper[j : j + 1, :]
        factor = jnp.where(row[:, :1] > j, upper[:, j : j + 1] / pivot[:, j : j + 1], 0.0)
        upper = upper - factor * pivot
        inverse = inverse - factor * inverse[j : j + 1, :]
    scale = lax.rsqrt(jnp.sum(eye * upper, axis=1, keepdims=True))
    upper = jnp.where(col >= row, upper * scale, 0.0)
    lower = dot(upper, eye, TN, HIGH)
    return inverse * scale, lower


def combination(sums, basis_gram, rows):
    width, total = sums.shape
    scaled = sums / rows
    square, coef = scaled[:, :width], scaled[:, width:]
    span = total - width
    twice = (
        lax.broadcasted_iota(jnp.int32, (span, span), 0)
        == lax.broadcasted_iota(jnp.int32, (span, span), 1)
    )
    inner = jnp.where(twice, 2.0, 0.0) - basis_gram / rows
    gram = square - dot(dot(coef, inner, NN, HIGH), coef, NT, HIGH)
    inverse, lower = eliminate(gram)
    row = lax.broadcasted_iota(jnp.int32, (width, total), 0)
    col = lax.broadcasted_iota(jnp.int32, (width, total), 1)
    weights = dot(inverse, jnp.where(col < width, (row == col).astype(F32), -scaled), NN, HIGH)
    return weights, lower


def self_products(values):
    high, low = split(values)
    return dot(high, high, NT) + dot(high, low, NT) + dot(low, high, NT)


def combine(weights, values):
    width = weights.shape[0]
    high, low = split(values)
    top, bottom = split(weights)
    first = dot(jnp.concatenate([top, bottom], 0), high, NN)
    return first[:width] + first[width:] + dot(top, low, NN)


def kernel(
    n_sta, n_cel, plane, height, cell_plane, depth, density, before, now, right_before,
    rights, left, alphas, betas,
    g_high, g_low, fs, c_square, c_top, lhs, gp, forward, rhs, z_right, z_left,
    send_sta, send_cel, w_full, v_full, station_buf, cell_buf, small_right, small_left,
    sta_send, sta_recv, cel_send, cel_recv, sr_send, sr_recv, sl_send, sl_recv,
):
    width, s_dev = now.shape
    c_dev = right_before.shape[1]
    places = {"sta": (lax.axis_index("sta"), n_sta), "cel": (lax.axis_index("cel"), n_cel)}
    cells = float(c_dev * n_cel)
    stations = float(s_dev * n_sta)

    def group(axis):
        me, n = places[axis]
        return [(o, lax.rem(me + o, n)) for o in range(1, n)]

    barrier = pltpu.get_barrier_semaphore()
    for axis in ("sta", "cel"):
        for _, peer in group(axis):
            pl.semaphore_signal(barrier, inc=1, device_id={axis: peer}, device_id_type=MESH)

    def send(axis, o, peer, source, target, sent, received):
        copy = pltpu.make_async_remote_copy(
            src_ref=source, dst_ref=target, send_sem=sent.at[o], recv_sem=received.at[o],
            device_id={axis: peer}, device_id_type=MESH)
        copy.start()
        return copy

    def finish(copies):
        for copy in copies:
            copy.wait()

    def columns(axis, index, extent):
        share = extent // places[axis][1]
        return pl.ds(pl.multiple_of(index * share, 128), share)

    def scatter(axis, step, source, buf, sent, received, produce, half_way):
        me, n = places[axis]
        copies, made, weights = [], [], None
        for position, (o, peer) in enumerate(group(axis) + [(0, me)]):
            span = columns(axis, peer, source.shape[1])
            if produce is not None:
                produce(span)
            made.append((o, peer, span))
            if position < n // 2 and half_way is not None:
                continue
            if weights is None and half_way is not None:
                weights = half_way()
            for o, peer, span in made:
                if weights is not None:
                    values, mixed = weights
                    source[:, span] = combine(mixed, values[:, span])
                if o:
                    copies.append(send(
                        axis, o, peer, source.at[:, span], buf.at[step, me],
                        sent.at[step, 0], received.at[step, 0]))
            made = []
        return copies

    def gather(axis, step, copies, source, full, buf, sent, received):
        me, n = places[axis]
        mine = columns(axis, me, source.shape[1])
        finish(copies)
        total = source[:, mine]
        for o, peer in group(axis):
            total = total + buf[step, peer]
        if axis == "sta":
            total = total * (GAIN * density[:, mine])
        full[step, :, mine] = total
        block = full.at[step, :, mine]
        finish([
            send(axis, o, peer, block, block, sent.at[step, 1], received.at[step, 1])
            for o, peer in group(axis)
        ])

    def small_start(axis, step, z, buf, sent, received):
        me, n = places[axis]
        rows = z.shape[0]
        buf[step, me, :rows, :rows] = self_products(z)
        block = buf.at[step, me]
        return [send(axis, o, peer, block, block, sent.at[step], received.at[step]) for o, peer in group(axis)]

    def small_end(copies, step, rows, buf, count):
        finish(copies)
        total = buf[step, 0, :rows, :rows]
        for index in range(1, buf.shape[1]):
            total = total + buf[step, index, :rows, :rows]
        return combination(total[:width], total[width:, width:], count)

    station_features(fs, plane, height)
    cell_features(c_square, c_top, cell_plane, depth)
    high, low = split(now[...])
    lhs[:width], lhs[2 * width : 3 * width] = high, low
    high, low = split(before[...])
    lhs[width : 2 * width], lhs[3 * width :] = high, low
    gp[...] = jnp.zeros_like(gp)
    s_tile, c_tile = 256, 512

    def make_rows(index, carry):
        rows = pl.ds(pl.multiple_of(index * s_tile, s_tile), s_tile)
        feature = fs[:, rows].astype(BF16)
        for start in range(0, c_dev, c_tile):
            cols = slice(start, start + c_tile)
            square = dot(feature, c_square[:, cols].astype(BF16), TN)
            top = dot(feature, c_top[:, cols].astype(BF16), TN)
            inverse = lax.rsqrt(square)
            two = inverse * inverse
            high, low = split(two * two * (top * inverse))
            g_high[rows, cols] = high
            g_low[rows, cols] = low
            first = dot(lhs[:, rows], high, NN)
            gp[: 2 * width, cols] += (
                first[: 2 * width] + first[2 * width :] + dot(lhs[: 2 * width, rows], low, NN)
            )
        return carry

    lax.fori_loop(0, s_dev // s_tile, make_rows, 0)
    send_sta[...] = gp[:width]
    gp[2 * width :] = gp[:width]
    pl.semaphore_wait(barrier, n_sta + n_cel - 2)
    copies = scatter("sta", 0, send_sta, station_buf, sta_send, sta_recv, None, None)

    for step in range(STEPS):
        gather("sta", step, copies, send_sta, w_full, station_buf, sta_send, sta_recv)
        w = w_full[step]
        z_right[:width] = w
        if step == 0:
            z_right[width : 2 * width] = right_before[...]
        r_rows = (step + 2) * width
        small = small_start("cel", step, z_right[:r_rows], small_right, sr_send, sr_recv)
        gained = GAIN * density[...]
        high, low = split(w * gained)
        rhs[:width], rhs[2 * width : 3 * width] = high, low
        if step == 0:
            high, low = split(right_before[...] * gained)
            rhs[width : 2 * width], rhs[3 * width :] = high, low

        def forward_share(span):
            first = dot(rhs[...], g_high[span, :], NT)
            second = dot(rhs[: 2 * width], g_low[span, :], NT)
            both = first[: 2 * width] + first[2 * width :] + second
            if step == 0:
                forward[: 2 * width, span] = both
            else:
                forward[:width, span] = both[:width]

        def right_half_way():
            weights, lower = small_end(small, step, r_rows, small_right, cells)
            alphas[step] = lower
            right = combine(weights, z_right[:r_rows])
            rights[step] = right
            if step + 1 < STEPS:
                z_right[r_rows : r_rows + width] = right
            return forward.at[:r_rows], weights

        copies = scatter(
            "cel", step, send_cel, cell_buf, cel_send, cel_recv, forward_share, right_half_way)
        if step + 1 < STEPS:
            forward[r_rows : r_rows + width] = send_cel[...]

        gather("cel", step, copies, send_cel, v_full, cell_buf, cel_send, cel_recv)
        v = v_full[step]
        z_left[:width] = v
        if step == 0:
            z_left[width : 2 * width] = before[...]
            z_left[2 * width : 3 * width] = now[...]
        l_rows = (step + 3) * width
        small = small_start("sta", step, z_left[:l_rows], small_left, sl_send, sl_recv)

        def left_half_way():
            weights, lower = small_end(small, step, l_rows, small_left, stations)
            betas[step] = lower
            block = combine(weights, z_left[:l_rows])
            if step + 1 < STEPS:
                z_left[l_rows : l_rows + width] = block
            else:
                left[...] = block
            return gp.at[:l_rows], weights

        if step + 1 == STEPS:
            left_half_way()
            break
        high, low = split(v)
        lhs[:width], lhs[width : 2 * width] = high, low

        def adjoint_share(span):
            first = dot(lhs[: 2 * width], g_high[:, span], NN)
            second = dot(lhs[:width], g_low[:, span], NN)
            gp[:width, span] = first[:width] + first[width:] + second

        copies = scatter(
            "sta", step + 1, send_sta, station_buf, sta_send, sta_recv, adjoint_share, left_half_way)
        if step + 2 < STEPS:
            gp[l_rows : l_rows + width] = send_sta[...]


def body(plane, height, cell_plane, depth, density, before, now, right_before):
    width, s_dev = now.shape
    c_dev = right_before.shape[1]
    n_sta = lax.axis_size("sta")
    n_cel = lax.axis_size("cel")
    vmem = pl.BlockSpec(memory_space=pltpu.VMEM)
    dma = pltpu.SemaphoreType.DMA
    lanes = 128
    out_shape = (
        jax.ShapeDtypeStruct((STEPS, width, c_dev), F32),
        jax.ShapeDtypeStruct((width, s_dev), F32),
        jax.ShapeDtypeStruct((STEPS, width, width), F32),
        jax.ShapeDtypeStruct((STEPS, width, width), F32),
    )
    scratch = [
        pltpu.VMEM((s_dev, c_dev), BF16),
        pltpu.VMEM((s_dev, c_dev), BF16),
        pltpu.VMEM((FEATURES, s_dev), F32),
        pltpu.VMEM((FEATURES, c_dev), F32),
        pltpu.VMEM((FEATURES, c_dev), F32),
        pltpu.VMEM((4 * width, s_dev), BF16),
        pltpu.VMEM(((STEPS + 1) * width, c_dev), F32),
        pltpu.VMEM(((STEPS + 1) * width, s_dev), F32),
        pltpu.VMEM((4 * width, c_dev), BF16),
        pltpu.VMEM(((STEPS + 1) * width, c_dev), F32),
        pltpu.VMEM(((STEPS + 2) * width, s_dev), F32),
        pltpu.VMEM((width, c_dev), F32),
        pltpu.VMEM((width, s_dev), F32),
        pltpu.VMEM((STEPS, width, c_dev), F32),
        pltpu.VMEM((STEPS, width, s_dev), F32),
        pltpu.VMEM((STEPS, n_sta, width, c_dev // n_sta), F32),
        pltpu.VMEM((STEPS, n_cel, width, s_dev // n_cel), F32),
        pltpu.VMEM((STEPS, n_cel, (STEPS + 1) * width, lanes), F32),
        pltpu.VMEM((STEPS, n_sta, (STEPS + 2) * width, lanes), F32),
        dma((STEPS, 2, n_sta)),
        dma((STEPS, 2, n_sta)),
        dma((STEPS, 2, n_cel)),
        dma((STEPS, 2, n_cel)),
        dma((STEPS, n_cel)),
        dma((STEPS, n_cel)),
        dma((STEPS, n_sta)),
        dma((STEPS, n_sta)),
    ]
    return pl.pallas_call(
        functools.partial(kernel, n_sta, n_cel),
        out_shape=out_shape,
        in_specs=[vmem] * 8,
        out_specs=(vmem,) * 4,
        scratch_shapes=scratch,
        compiler_params=pltpu.CompilerParams(
            collective_id=0, has_side_effects=True, vmem_limit_bytes=56 * 1024 * 1024
        ),
        cost_estimate=pl.CostEstimate(
            flops=2 * 3 * 2 * STEPS * width * s_dev * c_dev, bytes_accessed=4 * 1024 * 1024, transcendentals=s_dev * c_dev
        ),
    )(plane, height[None, :], cell_plane, depth[None, :], density[None, :], before, now, right_before)


def solution(mesh):
    in_specs = (
        P(None, "sta"),
        P("sta"),
        P(None, "cel"),
        P("cel"),
        P("cel"),
        P(None, "sta"),
        P(None, "sta"),
        P(None, "cel"),
    )
    out_specs = (P(None, None, "cel"), P(None, "sta"), P(), P())
    return jax.shard_map(body, mesh=mesh, in_specs=in_specs, out_specs=out_specs, check_vma=False)
```

```python
import functools

import jax
import jax.numpy as jnp
from jax import lax
from jax.experimental import pallas as pl
from jax.experimental.pallas import tpu as pltpu
from jax.sharding import PartitionSpec as P

STEPS = 2
GAIN = 4.0
CENTER = 96.0
FEATURES = 16
HIGH = lax.Precision.HIGHEST
F32 = jnp.float32
BF16 = jnp.bfloat16
MESH = pl.DeviceIdType.MESH
NN = (((1,), (0,)), ((), ()))
NT = (((1,), (1,)), ((), ()))
TN = (((0,), (0,)), ((), ()))


def dot(a, b, dims, precision=None):
    return lax.dot_general(a, b, dims, precision=precision, preferred_element_type=F32)


def split(values):
    high = values.astype(BF16)
    return high, (values - high.astype(F32)).astype(BF16)


def fill_features(ref, rows):
    for index, row in enumerate(rows):
        ref[index : index + 1, :] = row
    ref[len(rows) :, :] = jnp.zeros((FEATURES - len(rows), ref.shape[1]), F32)


def coordinates(plane, level):
    x = plane[0:1, :].astype(F32) - CENTER
    y = plane[1:2, :].astype(F32) - CENTER
    z = level[...].astype(F32)
    flat = x * x + y * y
    high = jnp.floor(flat / 256.0) * 256.0
    return x, y, z, high, flat - high, jnp.ones_like(x)


def station_features(ref, plane, height):
    x, y, z, high, low, one = coordinates(plane, height)
    fill_features(ref, [high, low, one, one, x, y, z * z, z, one, one])


def cell_features(square, top, plane, depth):
    x, y, z, high, low, one = coordinates(plane, depth)
    inner = z * z + z
    rows = [one, one, high, low, -2.0 * x, -2.0 * y, one, 2.0 * z + one, inner, 0.25 * one]
    fill_features(square, rows)
    rows = [-one, -one, -high, -low, 2.0 * x, 2.0 * y, 2.0 * one, 4.0 * z + 2.0 * one]
    fill_features(top, rows + [2.0 * inner, 0.5 * one])


def eliminate(gram):
    width = gram.shape[0]
    row = lax.broadcasted_iota(jnp.int32, (width, width), 0)
    col = lax.broadcasted_iota(jnp.int32, (width, width), 1)
    eye = (row == col).astype(F32)
    upper, inverse = gram, eye
    for j in range(width - 1):
        pivot = upper[j : j + 1, :]
        factor = jnp.where(row[:, :1] > j, upper[:, j : j + 1] / pivot[:, j : j + 1], 0.0)
        upper = upper - factor * pivot
        inverse = inverse - factor * inverse[j : j + 1, :]
    scale = lax.rsqrt(jnp.sum(eye * upper, axis=1, keepdims=True))
    upper = jnp.where(col >= row, upper * scale, 0.0)
    lower = dot(upper, eye, TN, HIGH)
    return inverse * scale, lower


def combination(sums, basis_gram, rows):
    width, total = sums.shape
    scaled = sums / rows
    square, coef = scaled[:, :width], scaled[:, width:]
    span = total - width
    twice = (
        lax.broadcasted_iota(jnp.int32, (span, span), 0)
        == lax.broadcasted_iota(jnp.int32, (span, span), 1)
    )
    inner = jnp.where(twice, 2.0, 0.0) - basis_gram / rows
    gram = square - dot(dot(coef, inner, NN, HIGH), coef, NT, HIGH)
    inverse, lower = eliminate(gram)
    row = lax.broadcasted_iota(jnp.int32, (width, total), 0)
    col = lax.broadcasted_iota(jnp.int32, (width, total), 1)
    weights = dot(inverse, jnp.where(col < width, (row == col).astype(F32), -scaled), NN, HIGH)
    return weights, lower


def products(values, count):
    high, low = split(values)
    return dot(high[:count], high, NT) + dot(high[:count], low, NT) + dot(low[:count], high, NT)


def grow(gram, weights, cross, rows):
    width, span = cross.shape
    basis = gram[:span, :span]
    side = dot(weights[:, :width], cross, NN, HIGH) + dot(weights[:, width:], basis, NN, HIGH)
    edge = span + width
    row = lax.broadcasted_iota(jnp.int32, (span, span), 0)
    col = lax.broadcasted_iota(jnp.int32, (span, span), 1)
    eye = (row == col).astype(F32)
    gram[span:edge, :span] = side
    gram[:span, span:edge] = dot(eye, side, NT, HIGH)
    gram[span:edge, span:edge] = eye[:width, :width] * rows


def combine(weights, values):
    width = weights.shape[0]
    high, low = split(values)
    top, bottom = split(weights)
    first = dot(jnp.concatenate([top, bottom], 0), high, NN)
    return first[:width] + first[width:] + dot(top, low, NN)


def kernel(
    n_sta, n_cel, plane, height, cell_plane, depth, density, before, now, right_before,
    rights, left, alphas, betas,
    g_high, g_low, fs, c_square, c_top, lhs, gp, forward, rhs, z_right, z_left,
    send_sta, send_cel, w_full, v_full, station_buf, cell_buf, small_right, small_share, small_left,
    gram_right, gram_left,
    sta_send, sta_recv, cel_send, cel_recv, sr_send, sr_recv, ss_send, ss_recv, sl_send, sl_recv,
):
    width, s_dev = now.shape
    c_dev = right_before.shape[1]
    places = {"sta": (lax.axis_index("sta"), n_sta), "cel": (lax.axis_index("cel"), n_cel)}
    cells = float(c_dev * n_cel)
    stations = float(s_dev * n_sta)

    def group(axis):
        me, n = places[axis]
        return [(o, lax.rem(me + o, n)) for o in range(1, n)]

    barrier = pltpu.get_barrier_semaphore()
    for axis in ("sta", "cel"):
        for _, peer in group(axis):
            pl.semaphore_signal(barrier, inc=1, device_id={axis: peer}, device_id_type=MESH)

    def send(axis, o, peer, source, target, sent, received):
        copy = pltpu.make_async_remote_copy(
            src_ref=source, dst_ref=target, send_sem=sent.at[o], recv_sem=received.at[o],
            device_id={axis: peer}, device_id_type=MESH)
        copy.start()
        return copy

    def finish(copies):
        for copy in copies:
            copy.wait()

    def columns(axis, index, extent):
        share = extent // places[axis][1]
        return pl.ds(pl.multiple_of(index * share, 128), share)

    def scatter(axis, step, source, buf, sent, received, produce, half_way):
        me, n = places[axis]
        copies, made, weights = [], [], None
        for position, (o, peer) in enumerate(group(axis) + [(0, me)]):
            span = columns(axis, peer, source.shape[1])
            if produce is not None:
                produce(span)
            made.append((o, peer, span))
            if position < n // 2 and half_way is not None:
                continue
            if weights is None and half_way is not None:
                weights = half_way()
            for o, peer, span in made:
                if weights is not None:
                    values, mixed = weights
                    source[:, span] = combine(mixed, values[:, span])
                if o:
                    copies.append(send(
                        axis, o, peer, source.at[:, span], buf.at[step, me],
                        sent.at[step, 0], received.at[step, 0]))
            made = []
        return copies

    def reduced(axis, step, copies, source, buf):
        me, n = places[axis]
        finish(copies)
        total = source[:, columns(axis, me, source.shape[1])]
        for o, peer in group(axis):
            total = total + buf[step, peer]
        return total

    def gather(axis, step, full, total, sent, received):
        span = columns(axis, places[axis][0], full.shape[2])
        full[step, :, span] = total
        block = full.at[step, :, span]
        return [
            send(axis, o, peer, block, block, sent.at[step, 1], received.at[step, 1])
            for o, peer in group(axis)
        ]

    def exchange(axis, step, values, buf, sent, received):
        me, n = places[axis]
        rows, cols = values.shape
        buf[step, me, :rows, :cols] = values
        block = buf.at[step, me, :rows]
        return [
            send(axis, o, peer, block, block, sent.at[step], received.at[step])
            for o, peer in group(axis)
        ]

    def collect(copies, step, rows, cols, buf):
        finish(copies)
        total = buf[step, 0, :rows, :cols]
        for index in range(1, buf.shape[1]):
            total = total + buf[step, index, :rows, :cols]
        return total

    def solve(step, sums, gram, count, lowers):
        span = sums.shape[1] - width
        if step == 0:
            gram[:span, :span] = sums[width:, width:]
        weights, lowers[step] = combination(sums[:width], gram[:span, :span], count)
        return weights

    station_features(fs, plane, height)
    cell_features(c_square, c_top, cell_plane, depth)
    high, low = split(now[...])
    lhs[:width], lhs[2 * width : 3 * width] = high, low
    high, low = split(before[...])
    lhs[width : 2 * width], lhs[3 * width :] = high, low
    gp[...] = jnp.zeros_like(gp)
    s_tile, c_tile = 256, 512

    def make_rows(index, carry):
        rows = pl.ds(pl.multiple_of(index * s_tile, s_tile), s_tile)
        feature = fs[:, rows].astype(BF16)
        for start in range(0, c_dev, c_tile):
            cols = slice(start, start + c_tile)
            square = dot(feature, c_square[:, cols].astype(BF16), TN)
            top = dot(feature, c_top[:, cols].astype(BF16), TN)
            inverse = lax.rsqrt(square)
            two = inverse * inverse
            high, low = split(two * two * (top * inverse))
            g_high[rows, cols] = high
            g_low[rows, cols] = low
            first = dot(lhs[:, rows], high, NN)
            gp[: 2 * width, cols] += (
                first[: 2 * width] + first[2 * width :] + dot(lhs[: 2 * width, rows], low, NN)
            )
        return carry

    lax.fori_loop(0, s_dev // s_tile, make_rows, 0)
    send_sta[...] = gp[:width]
    gp[2 * width :] = gp[:width]
    pl.semaphore_wait(barrier, n_sta + n_cel - 2)
    copies = scatter("sta", 0, send_sta, station_buf, sta_send, sta_recv, None, None)

    c_me = places["cel"][0]
    for step in range(STEPS):
        last = step + 1 == STEPS
        total = reduced("sta", step, copies, send_sta, station_buf)
        total = total * (GAIN * density[:, columns("sta", places["sta"][0], c_dev)])
        finish(gather("sta", step, w_full, total, sta_send, sta_recv))
        w = w_full[step]
        z_right[:width] = w
        if step == 0:
            z_right[width : 2 * width] = right_before[...]
        r_rows = (step + 2) * width
        r_sent = width if step else r_rows
        small = exchange(
            "cel", step, products(z_right[:r_rows], r_sent), small_right, sr_send, sr_recv)
        gained = GAIN * density[...]
        high, low = split(w * gained)
        rhs[:width], rhs[2 * width : 3 * width] = high, low
        if step == 0:
            high, low = split(right_before[...] * gained)
            rhs[width : 2 * width], rhs[3 * width :] = high, low

        def forward_share(span):
            first = dot(rhs[...], g_high[span, :], NT)
            second = dot(rhs[: 2 * width], g_low[span, :], NT)
            both = first[: 2 * width] + first[2 * width :] + second
            if step == 0:
                forward[: 2 * width, span] = both
            else:
                forward[:width, span] = both[:width]

        right_sums = []

        def right_half_way():
            sums = collect(small, step, r_sent, r_rows, small_right)
            right_sums.append(sums)
            weights = solve(step, sums, gram_right, cells, alphas)
            right_sums.append(weights)
            return forward.at[:r_rows], weights

        copies = scatter(
            "cel", step, send_cel, cell_buf, cel_send, cel_recv, forward_share, right_half_way)
        sums, weights = right_sums
        right = combine(weights, z_right[:r_rows])
        rights[step] = right
        if not last:
            z_right[r_rows : r_rows + width] = right
            forward[r_rows : r_rows + width] = send_cel[...]
            grow(gram_right, weights, sums[:width, width:], cells)
        if step == 0:
            z_left[width : 2 * width] = before[...]
            z_left[2 * width : 3 * width] = now[...]

        total = reduced("cel", step, copies, send_cel, cell_buf)
        mine = columns("cel", c_me, s_dev)
        z_left[:width, mine] = total
        l_rows = (step + 3) * width
        l_sent = width if step else l_rows
        shared = exchange(
            "cel", step, products(z_left[:l_rows, mine], l_sent), small_share, ss_send, ss_recv)
        arriving = gather("cel", step, v_full, total, cel_send, cel_recv)

        def left_exchange():
            sums = collect(shared, step, l_sent, l_rows, small_share)
            return exchange("sta", step, sums, small_left, sl_send, sl_recv)

        if last:
            small = left_exchange()
            finish(arriving)
            z_left[:width] = v_full[step]
            sums = collect(small, step, l_sent, l_rows, small_left)
            left[...] = combine(solve(step, sums, gram_left, stations, betas), z_left[:l_rows])
            break

        def adjoint(rows, span):
            first = dot(lhs[: 2 * width, rows], g_high[rows, span], NN)
            return first[:width] + first[width:] + dot(lhs[:width, rows], g_low[rows, span], NN)

        def load(rows):
            high, low = split(v_full[step, :, rows])
            lhs[:width, rows], lhs[width : 2 * width, rows] = high, low

        load(mine)
        for start in range(0, c_dev, c_tile):
            span = slice(start, start + c_tile)
            gp[:width, span] = adjoint(mine, span)
        small = left_exchange()
        rows = mine
        for o, copy in enumerate(arriving, 1):
            copy.wait()
            rows = columns("cel", lax.rem(c_me + n_cel - o, n_cel), s_dev)
            load(rows)
            if o + 1 < n_cel:
                for start in range(0, c_dev, c_tile):
                    span = slice(start, start + c_tile)
                    gp[:width, span] += adjoint(rows, span)
        z_left[:width] = v_full[step]

        def adjoint_share(span):
            gp[:width, span] += adjoint(rows, span)

        left_sums = []

        def left_half_way():
            sums = collect(small, step, l_sent, l_rows, small_left)
            left_sums.append(sums)
            weights = solve(step, sums, gram_left, stations, betas)
            left_sums.append(weights)
            return gp.at[:l_rows], weights

        copies = scatter(
            "sta", step + 1, send_sta, station_buf, sta_send, sta_recv, adjoint_share, left_half_way)
        sums, weights = left_sums
        z_left[l_rows : l_rows + width] = combine(weights, z_left[:l_rows])
        grow(gram_left, weights, sums[:width, width:], stations)
        if step + 2 < STEPS:
            gp[l_rows : l_rows + width] = send_sta[...]


def body(plane, height, cell_plane, depth, density, before, now, right_before):
    width, s_dev = now.shape
    c_dev = right_before.shape[1]
    n_sta = lax.axis_size("sta")
    n_cel = lax.axis_size("cel")
    vmem = pl.BlockSpec(memory_space=pltpu.VMEM)
    dma = pltpu.SemaphoreType.DMA
    lanes = 128
    out_shape = (
        jax.ShapeDtypeStruct((STEPS, width, c_dev), F32),
        jax.ShapeDtypeStruct((width, s_dev), F32),
        jax.ShapeDtypeStruct((STEPS, width, width), F32),
        jax.ShapeDtypeStruct((STEPS, width, width), F32),
    )
    scratch = [
        pltpu.VMEM((s_dev, c_dev), BF16),
        pltpu.VMEM((s_dev, c_dev), BF16),
        pltpu.VMEM((FEATURES, s_dev), F32),
        pltpu.VMEM((FEATURES, c_dev), F32),
        pltpu.VMEM((FEATURES, c_dev), F32),
        pltpu.VMEM((4 * width, s_dev), BF16),
        pltpu.VMEM(((STEPS + 1) * width, c_dev), F32),
        pltpu.VMEM(((STEPS + 1) * width, s_dev), F32),
        pltpu.VMEM((4 * width, c_dev), BF16),
        pltpu.VMEM(((STEPS + 1) * width, c_dev), F32),
        pltpu.VMEM(((STEPS + 2) * width, s_dev), F32),
        pltpu.VMEM((width, c_dev), F32),
        pltpu.VMEM((width, s_dev), F32),
        pltpu.VMEM((STEPS, width, c_dev), F32),
        pltpu.VMEM((STEPS, width, s_dev), F32),
        pltpu.VMEM((STEPS, n_sta, width, c_dev // n_sta), F32),
        pltpu.VMEM((STEPS, n_cel, width, s_dev // n_cel), F32),
        pltpu.VMEM((STEPS, n_cel, (STEPS + 1) * width, lanes), F32),
        pltpu.VMEM((STEPS, n_cel, (STEPS + 2) * width, lanes), F32),
        pltpu.VMEM((STEPS, n_sta, (STEPS + 2) * width, lanes), F32),
        pltpu.VMEM(((STEPS + 1) * width, lanes), F32),
        pltpu.VMEM(((STEPS + 2) * width, lanes), F32),
        dma((STEPS, 2, n_sta)),
        dma((STEPS, 2, n_sta)),
        dma((STEPS, 2, n_cel)),
        dma((STEPS, 2, n_cel)),
        dma((STEPS, n_cel)),
        dma((STEPS, n_cel)),
        dma((STEPS, n_cel)),
        dma((STEPS, n_cel)),
        dma((STEPS, n_sta)),
        dma((STEPS, n_sta)),
    ]
    return pl.pallas_call(
        functools.partial(kernel, n_sta, n_cel),
        out_shape=out_shape,
        in_specs=[vmem] * 8,
        out_specs=(vmem,) * 4,
        scratch_shapes=scratch,
        compiler_params=pltpu.CompilerParams(
            collective_id=0, has_side_effects=True, vmem_limit_bytes=56 * 1024 * 1024
        ),
        cost_estimate=pl.CostEstimate(
            flops=2 * 3 * 2 * STEPS * width * s_dev * c_dev, bytes_accessed=4 * 1024 * 1024, transcendentals=s_dev * c_dev
        ),
    )(plane, height[None, :], cell_plane, depth[None, :], density[None, :], before, now, right_before)


def solution(mesh):
    in_specs = (
        P(None, "sta"),
        P("sta"),
        P(None, "cel"),
        P("cel"),
        P("cel"),
        P(None, "sta"),
        P(None, "sta"),
        P(None, "cel"),
    )
    out_specs = (P(None, None, "cel"), P(None, "sta"), P(), P())
    return jax.shard_map(body, mesh=mesh, in_specs=in_specs, out_specs=out_specs, check_vma=False)
```

```python
import functools

import jax
import jax.numpy as jnp
from jax import lax
from jax.experimental import pallas as pl
from jax.experimental.pallas import tpu as pltpu
from jax.sharding import PartitionSpec as P

STEPS = 2
GAIN = 4.0
CENTER = 96.0
FEATURES = 16
HIGH = lax.Precision.HIGHEST
F32 = jnp.float32
BF16 = jnp.bfloat16
MESH = pl.DeviceIdType.MESH
NN = (((1,), (0,)), ((), ()))
NT = (((1,), (1,)), ((), ()))
TN = (((0,), (0,)), ((), ()))


def dot(a, b, dims, precision=None):
    return lax.dot_general(a, b, dims, precision=precision, preferred_element_type=F32)


def split(values):
    high = values.astype(BF16)
    return high, (values - high.astype(F32)).astype(BF16)


def fill_features(ref, rows):
    for index, row in enumerate(rows):
        ref[index : index + 1, :] = row
    ref[len(rows) :, :] = jnp.zeros((FEATURES - len(rows), ref.shape[1]), F32)


def coordinates(plane, level):
    x = plane[0:1, :].astype(F32) - CENTER
    y = plane[1:2, :].astype(F32) - CENTER
    z = level[...].astype(F32)
    flat = x * x + y * y
    high = jnp.floor(flat / 256.0) * 256.0
    return x, y, z, high, flat - high, jnp.ones_like(x)


def station_features(ref, plane, height):
    x, y, z, high, low, one = coordinates(plane, height)
    fill_features(ref, [high, low, one, one, x, y, z * z, z, one, one])


def cell_features(square, top, plane, depth):
    x, y, z, high, low, one = coordinates(plane, depth)
    inner = z * z + z
    rows = [one, one, high, low, -2.0 * x, -2.0 * y, one, 2.0 * z + one, inner, 0.25 * one]
    fill_features(square, rows)
    rows = [-one, -one, -high, -low, 2.0 * x, 2.0 * y, 2.0 * one, 4.0 * z + 2.0 * one]
    fill_features(top, rows + [2.0 * inner, 0.5 * one])


def eliminate(gram):
    width = gram.shape[0]
    row = lax.broadcasted_iota(jnp.int32, (width, width), 0)
    col = lax.broadcasted_iota(jnp.int32, (width, width), 1)
    eye = (row == col).astype(F32)
    upper, inverse = gram, eye
    for j in range(width - 1):
        pivot = upper[j : j + 1, :]
        factor = jnp.where(row[:, :1] > j, upper[:, j : j + 1] / pivot[:, j : j + 1], 0.0)
        upper = upper - factor * pivot
        inverse = inverse - factor * inverse[j : j + 1, :]
    scale = lax.rsqrt(jnp.sum(eye * upper, axis=1, keepdims=True))
    upper = jnp.where(col >= row, upper * scale, 0.0)
    lower = dot(upper, eye, TN, HIGH)
    return inverse * scale, lower


def combination(sums, basis_gram, rows):
    width, total = sums.shape
    scaled = sums / rows
    square, coef = scaled[:, :width], scaled[:, width:]
    span = total - width
    twice = (
        lax.broadcasted_iota(jnp.int32, (span, span), 0)
        == lax.broadcasted_iota(jnp.int32, (span, span), 1)
    )
    inner = jnp.where(twice, 2.0, 0.0) - basis_gram / rows
    gram = square - dot(dot(coef, inner, NN, HIGH), coef, NT, HIGH)
    inverse, lower = eliminate(gram)
    row = lax.broadcasted_iota(jnp.int32, (width, total), 0)
    col = lax.broadcasted_iota(jnp.int32, (width, total), 1)
    weights = dot(inverse, jnp.where(col < width, (row == col).astype(F32), -scaled), NN, HIGH)
    return weights, lower


def products(values, count):
    high, low = split(values)
    return dot(high[:count], high, NT) + dot(high[:count], low, NT) + dot(low[:count], high, NT)


def grow(gram, weights, cross, rows):
    width, span = cross.shape
    basis = gram[:span, :span]
    side = dot(weights[:, :width], cross, NN, HIGH) + dot(weights[:, width:], basis, NN, HIGH)
    edge = span + width
    row = lax.broadcasted_iota(jnp.int32, (span, span), 0)
    col = lax.broadcasted_iota(jnp.int32, (span, span), 1)
    eye = (row == col).astype(F32)
    gram[span:edge, :span] = side
    gram[:span, span:edge] = dot(eye, side, NT, HIGH)
    gram[span:edge, span:edge] = eye[:width, :width] * rows


def combine(weights, values):
    width = weights.shape[0]
    high, low = split(values)
    top, bottom = split(weights)
    first = dot(jnp.concatenate([top, bottom], 0), high, NN)
    return first[:width] + first[width:] + dot(top, low, NN)


def kernel(
    n_sta, n_cel, plane, height, cell_plane, depth, density, before, now, right_before,
    rights, left, alphas, betas,
    g_high, g_low, fs, c_square, c_top, lhs, gp, forward, rhs, z_right, z_left,
    send_sta, send_cel, w_full, v_full, station_buf, cell_buf, small_right, small_share, small_left,
    gram_right, gram_left,
    sta_send, sta_recv, cel_send, cel_recv, sr_send, sr_recv, ss_send, ss_recv, sl_send, sl_recv,
):
    width, s_dev = now.shape
    c_dev = right_before.shape[1]
    places = {"sta": (lax.axis_index("sta"), n_sta), "cel": (lax.axis_index("cel"), n_cel)}
    cells = float(c_dev * n_cel)
    stations = float(s_dev * n_sta)

    def group(axis):
        me, n = places[axis]
        return [(o, lax.rem(me + o, n)) for o in range(1, n)]

    barrier = pltpu.get_barrier_semaphore()
    for axis in ("sta", "cel"):
        for _, peer in group(axis):
            pl.semaphore_signal(barrier, inc=1, device_id={axis: peer}, device_id_type=MESH)

    def send(axis, o, peer, source, target, sent, received):
        copy = pltpu.make_async_remote_copy(
            src_ref=source, dst_ref=target, send_sem=sent.at[o], recv_sem=received.at[o],
            device_id={axis: peer}, device_id_type=MESH)
        copy.start()
        return copy

    def finish(copies):
        for copy in copies:
            copy.wait()

    def columns(axis, index, extent):
        share = extent // places[axis][1]
        return pl.ds(pl.multiple_of(index * share, 128), share)

    def scatter(axis, step, source, buf, sent, received, produce, half_way):
        me, n = places[axis]
        copies, made, weights = [], [], None
        for position, (o, peer) in enumerate(group(axis) + [(0, me)]):
            span = columns(axis, peer, source.shape[1])
            if produce is not None:
                produce(span)
            made.append((o, peer, span))
            if position < n // 2 and half_way is not None:
                continue
            if weights is None and half_way is not None:
                weights = half_way()
            for o, peer, span in made:
                if weights is not None:
                    values, mixed = weights
                    source[:, span] = combine(mixed, values[:, span])
                if o:
                    copies.append(send(
                        axis, o, peer, source.at[:, span], buf.at[step, me],
                        sent.at[step, 0], received.at[step, 0]))
            made = []
        return copies

    def reduced(axis, step, copies, source, buf):
        me, n = places[axis]
        finish(copies)
        total = source[:, columns(axis, me, source.shape[1])]
        for o, peer in group(axis):
            total = total + buf[step, peer]
        return total

    def gather(axis, step, full, total, sent, received):
        span = columns(axis, places[axis][0], full.shape[2])
        full[step, :, span] = total
        block = full.at[step, :, span]
        return [
            send(axis, o, peer, block, block, sent.at[step, 1], received.at[step, 1])
            for o, peer in group(axis)
        ]

    def exchange(axis, step, values, buf, sent, received):
        me, n = places[axis]
        rows, cols = values.shape
        buf[step, me, :rows, :cols] = values
        block = buf.at[step, me, :rows]
        return [
            send(axis, o, peer, block, block, sent.at[step], received.at[step])
            for o, peer in group(axis)
        ]

    def collect(copies, step, rows, cols, buf):
        finish(copies)
        total = buf[step, 0, :rows, :cols]
        for index in range(1, buf.shape[1]):
            total = total + buf[step, index, :rows, :cols]
        return total

    def solve(step, sums, gram, count, lowers):
        span = sums.shape[1] - width
        if step == 0:
            gram[:span, :span] = sums[width:, width:]
        weights, lowers[step] = combination(sums[:width], gram[:span, :span], count)
        return weights

    station_features(fs, plane, height)
    cell_features(c_square, c_top, cell_plane, depth)
    high, low = split(now[...])
    lhs[:width], lhs[2 * width : 3 * width] = high, low
    high, low = split(before[...])
    lhs[width : 2 * width], lhs[3 * width :] = high, low
    gp[...] = jnp.zeros_like(gp)
    s_tile, c_tile, g_tile, g_chunk = 256, 512, 256, 32

    def make_rows(index, carry):
        rows = pl.ds(pl.multiple_of(index * s_tile, s_tile), s_tile)
        feature = fs[:, rows].astype(BF16)

        def multiply(cols):
            first = dot(lhs[:, rows], g_high[rows, cols], NN)
            gp[: 2 * width, cols] += (
                first[: 2 * width]
                + first[2 * width :]
                + dot(lhs[: 2 * width, rows], g_low[rows, cols], NN)
            )

        previous = None
        for start in range(0, c_dev, g_tile):
            cols = slice(start, start + g_tile)
            square = dot(feature, c_square[:, cols].astype(BF16), TN)
            top = dot(feature, c_top[:, cols].astype(BF16), TN)
            for chunk in range(0, s_tile, g_chunk):
                part = slice(chunk, chunk + g_chunk)
                inverse = lax.rsqrt(square[part])
                two = inverse * inverse
                high, low = split(two * two * (top[part] * inverse))
                at = pl.ds(pl.multiple_of(index * s_tile + chunk, g_chunk), g_chunk)
                g_high[at, cols] = high
                g_low[at, cols] = low
            if previous is not None:
                multiply(previous)
            previous = cols
        multiply(previous)
        return carry

    lax.fori_loop(0, s_dev // s_tile, make_rows, 0)
    send_sta[...] = gp[:width]
    gp[2 * width :] = gp[:width]
    pl.semaphore_wait(barrier, n_sta + n_cel - 2)
    copies = scatter("sta", 0, send_sta, station_buf, sta_send, sta_recv, None, None)

    c_me = places["cel"][0]
    for step in range(STEPS):
        last = step + 1 == STEPS
        total = reduced("sta", step, copies, send_sta, station_buf)
        total = total * (GAIN * density[:, columns("sta", places["sta"][0], c_dev)])
        finish(gather("sta", step, w_full, total, sta_send, sta_recv))
        w = w_full[step]
        z_right[:width] = w
        if step == 0:
            z_right[width : 2 * width] = right_before[...]
        r_rows = (step + 2) * width
        r_sent = width if step else r_rows
        small = exchange(
            "cel", step, products(z_right[:r_rows], r_sent), small_right, sr_send, sr_recv)
        gained = GAIN * density[...]
        high, low = split(w * gained)
        rhs[:width], rhs[2 * width : 3 * width] = high, low
        if step == 0:
            high, low = split(right_before[...] * gained)
            rhs[width : 2 * width], rhs[3 * width :] = high, low

        def forward_share(span):
            first = dot(rhs[...], g_high[span, :], NT)
            second = dot(rhs[: 2 * width], g_low[span, :], NT)
            both = first[: 2 * width] + first[2 * width :] + second
            if step == 0:
                forward[: 2 * width, span] = both
            else:
                forward[:width, span] = both[:width]

        right_sums = []

        def right_half_way():
            sums = collect(small, step, r_sent, r_rows, small_right)
            right_sums.append(sums)
            weights = solve(step, sums, gram_right, cells, alphas)
            right_sums.append(weights)
            return forward.at[:r_rows], weights

        copies = scatter(
            "cel", step, send_cel, cell_buf, cel_send, cel_recv, forward_share, right_half_way)
        sums, weights = right_sums
        right = combine(weights, z_right[:r_rows])
        rights[step] = right
        if not last:
            z_right[r_rows : r_rows + width] = right
            forward[r_rows : r_rows + width] = send_cel[...]
            grow(gram_right, weights, sums[:width, width:], cells)
        if step == 0:
            z_left[width : 2 * width] = before[...]
            z_left[2 * width : 3 * width] = now[...]

        total = reduced("cel", step, copies, send_cel, cell_buf)
        mine = columns("cel", c_me, s_dev)
        z_left[:width, mine] = total
        l_rows = (step + 3) * width
        l_sent = width if step else l_rows
        shared = exchange(
            "cel", step, products(z_left[:l_rows, mine], l_sent), small_share, ss_send, ss_recv)
        arriving = gather("cel", step, v_full, total, cel_send, cel_recv)

        def left_exchange():
            sums = collect(shared, step, l_sent, l_rows, small_share)
            return exchange("sta", step, sums, small_left, sl_send, sl_recv)

        if last:
            small = left_exchange()
            finish(arriving)
            z_left[:width] = v_full[step]
            sums = collect(small, step, l_sent, l_rows, small_left)
            left[...] = combine(solve(step, sums, gram_left, stations, betas), z_left[:l_rows])
            break

        def adjoint(rows, span):
            first = dot(lhs[: 2 * width, rows], g_high[rows, span], NN)
            return first[:width] + first[width:] + dot(lhs[:width, rows], g_low[rows, span], NN)

        def load(rows):
            high, low = split(v_full[step, :, rows])
            lhs[:width, rows], lhs[width : 2 * width, rows] = high, low

        load(mine)
        for start in range(0, c_dev, c_tile):
            span = slice(start, start + c_tile)
            gp[:width, span] = adjoint(mine, span)
        small = left_exchange()
        rows = mine
        for o, copy in enumerate(arriving, 1):
            copy.wait()
            rows = columns("cel", lax.rem(c_me + n_cel - o, n_cel), s_dev)
            load(rows)
            if o + 1 < n_cel:
                for start in range(0, c_dev, c_tile):
                    span = slice(start, start + c_tile)
                    gp[:width, span] += adjoint(rows, span)
        z_left[:width] = v_full[step]

        def adjoint_share(span):
            gp[:width, span] += adjoint(rows, span)

        left_sums = []

        def left_half_way():
            sums = collect(small, step, l_sent, l_rows, small_left)
            left_sums.append(sums)
            weights = solve(step, sums, gram_left, stations, betas)
            left_sums.append(weights)
            return gp.at[:l_rows], weights

        copies = scatter(
            "sta", step + 1, send_sta, station_buf, sta_send, sta_recv, adjoint_share, left_half_way)
        sums, weights = left_sums
        z_left[l_rows : l_rows + width] = combine(weights, z_left[:l_rows])
        grow(gram_left, weights, sums[:width, width:], stations)
        if step + 2 < STEPS:
            gp[l_rows : l_rows + width] = send_sta[...]


def body(plane, height, cell_plane, depth, density, before, now, right_before):
    width, s_dev = now.shape
    c_dev = right_before.shape[1]
    n_sta = lax.axis_size("sta")
    n_cel = lax.axis_size("cel")
    vmem = pl.BlockSpec(memory_space=pltpu.VMEM)
    dma = pltpu.SemaphoreType.DMA
    lanes = 128
    out_shape = (
        jax.ShapeDtypeStruct((STEPS, width, c_dev), F32),
        jax.ShapeDtypeStruct((width, s_dev), F32),
        jax.ShapeDtypeStruct((STEPS, width, width), F32),
        jax.ShapeDtypeStruct((STEPS, width, width), F32),
    )
    scratch = [
        pltpu.VMEM((s_dev, c_dev), BF16),
        pltpu.VMEM((s_dev, c_dev), BF16),
        pltpu.VMEM((FEATURES, s_dev), F32),
        pltpu.VMEM((FEATURES, c_dev), F32),
        pltpu.VMEM((FEATURES, c_dev), F32),
        pltpu.VMEM((4 * width, s_dev), BF16),
        pltpu.VMEM(((STEPS + 1) * width, c_dev), F32),
        pltpu.VMEM(((STEPS + 1) * width, s_dev), F32),
        pltpu.VMEM((4 * width, c_dev), BF16),
        pltpu.VMEM(((STEPS + 1) * width, c_dev), F32),
        pltpu.VMEM(((STEPS + 2) * width, s_dev), F32),
        pltpu.VMEM((width, c_dev), F32),
        pltpu.VMEM((width, s_dev), F32),
        pltpu.VMEM((STEPS, width, c_dev), F32),
        pltpu.VMEM((STEPS, width, s_dev), F32),
        pltpu.VMEM((STEPS, n_sta, width, c_dev // n_sta), F32),
        pltpu.VMEM((STEPS, n_cel, width, s_dev // n_cel), F32),
        pltpu.VMEM((STEPS, n_cel, (STEPS + 1) * width, lanes), F32),
        pltpu.VMEM((STEPS, n_cel, (STEPS + 2) * width, lanes), F32),
        pltpu.VMEM((STEPS, n_sta, (STEPS + 2) * width, lanes), F32),
        pltpu.VMEM(((STEPS + 1) * width, lanes), F32),
        pltpu.VMEM(((STEPS + 2) * width, lanes), F32),
        dma((STEPS, 2, n_sta)),
        dma((STEPS, 2, n_sta)),
        dma((STEPS, 2, n_cel)),
        dma((STEPS, 2, n_cel)),
        dma((STEPS, n_cel)),
        dma((STEPS, n_cel)),
        dma((STEPS, n_cel)),
        dma((STEPS, n_cel)),
        dma((STEPS, n_sta)),
        dma((STEPS, n_sta)),
    ]
    return pl.pallas_call(
        functools.partial(kernel, n_sta, n_cel),
        out_shape=out_shape,
        in_specs=[vmem] * 8,
        out_specs=(vmem,) * 4,
        scratch_shapes=scratch,
        compiler_params=pltpu.CompilerParams(
            collective_id=0, has_side_effects=True, vmem_limit_bytes=56 * 1024 * 1024
        ),
        cost_estimate=pl.CostEstimate(
            flops=2 * 3 * 2 * STEPS * width * s_dev * c_dev, bytes_accessed=4 * 1024 * 1024, transcendentals=s_dev * c_dev
        ),
    )(plane, height[None, :], cell_plane, depth[None, :], density[None, :], before, now, right_before)


def solution(mesh):
    in_specs = (
        P(None, "sta"),
        P("sta"),
        P(None, "cel"),
        P("cel"),
        P("cel"),
        P(None, "sta"),
        P(None, "sta"),
        P(None, "cel"),
    )
    out_specs = (P(None, None, "cel"), P(None, "sta"), P(), P())
    return jax.shard_map(body, mesh=mesh, in_specs=in_specs, out_specs=out_specs, check_vma=False)
```

```python
import functools

import jax
import jax.numpy as jnp
from jax import lax
from jax.experimental import pallas as pl
from jax.experimental.pallas import tpu as pltpu
from jax.sharding import PartitionSpec as P

STEPS = 2
GAIN = 4.0
CENTER = 96.0
FEATURES = 16
HIGH = lax.Precision.HIGHEST
F32 = jnp.float32
BF16 = jnp.bfloat16
MESH = pl.DeviceIdType.MESH
NN = (((1,), (0,)), ((), ()))
NT = (((1,), (1,)), ((), ()))
TN = (((0,), (0,)), ((), ()))


def dot(a, b, dims, precision=None):
    return lax.dot_general(a, b, dims, precision=precision, preferred_element_type=F32)


def split(values):
    high = values.astype(BF16)
    return high, (values - high.astype(F32)).astype(BF16)


def fill_features(ref, rows):
    for index, row in enumerate(rows):
        ref[index : index + 1, :] = row
    ref[len(rows) :, :] = jnp.zeros((FEATURES - len(rows), ref.shape[1]), F32)


def coordinates(plane, level):
    x = plane[0:1, :].astype(F32) - CENTER
    y = plane[1:2, :].astype(F32) - CENTER
    z = level[...].astype(F32)
    flat = x * x + y * y
    high = jnp.floor(flat / 256.0) * 256.0
    return x, y, z, high, flat - high, jnp.ones_like(x)


def station_features(ref, plane, height):
    x, y, z, high, low, one = coordinates(plane, height)
    fill_features(ref, [high, low, one, one, x, y, z * z, z, one, one])


def cell_features(square, top, plane, depth):
    x, y, z, high, low, one = coordinates(plane, depth)
    inner = z * z + z
    rows = [one, one, high, low, -2.0 * x, -2.0 * y, one, 2.0 * z + one, inner, 0.25 * one]
    fill_features(square, rows)
    rows = [-one, -one, -high, -low, 2.0 * x, 2.0 * y, 2.0 * one, 4.0 * z + 2.0 * one]
    fill_features(top, rows + [2.0 * inner, 0.5 * one])


def eliminate(gram):
    width = gram.shape[0]
    row = lax.broadcasted_iota(jnp.int32, (width, width), 0)
    col = lax.broadcasted_iota(jnp.int32, (width, width), 1)
    eye = (row == col).astype(F32)
    upper, inverse = gram, eye
    for j in range(width - 1):
        pivot = upper[j : j + 1, :]
        factor = jnp.where(row[:, :1] > j, upper[:, j : j + 1] / pivot[:, j : j + 1], 0.0)
        upper = upper - factor * pivot
        inverse = inverse - factor * inverse[j : j + 1, :]
    scale = lax.rsqrt(jnp.sum(eye * upper, axis=1, keepdims=True))
    upper = jnp.where(col >= row, upper * scale, 0.0)
    lower = dot(upper, eye, TN, HIGH)
    return inverse * scale, lower


def combination(sums, basis_gram, rows):
    width, total = sums.shape
    scaled = sums / rows
    square, coef = scaled[:, :width], scaled[:, width:]
    span = total - width
    twice = (
        lax.broadcasted_iota(jnp.int32, (span, span), 0)
        == lax.broadcasted_iota(jnp.int32, (span, span), 1)
    )
    inner = jnp.where(twice, 2.0, 0.0) - basis_gram / rows
    gram = square - dot(dot(coef, inner, NN, HIGH), coef, NT, HIGH)
    inverse, lower = eliminate(gram)
    row = lax.broadcasted_iota(jnp.int32, (width, total), 0)
    col = lax.broadcasted_iota(jnp.int32, (width, total), 1)
    weights = dot(inverse, jnp.where(col < width, (row == col).astype(F32), -scaled), NN, HIGH)
    return weights, lower


def products(values, count):
    high, low = split(values)
    return dot(high[:count], high, NT) + dot(high[:count], low, NT) + dot(low[:count], high, NT)


def grow(gram, weights, cross, rows):
    width, span = cross.shape
    basis = gram[:span, :span]
    side = dot(weights[:, :width], cross, NN, HIGH) + dot(weights[:, width:], basis, NN, HIGH)
    edge = span + width
    row = lax.broadcasted_iota(jnp.int32, (span, span), 0)
    col = lax.broadcasted_iota(jnp.int32, (span, span), 1)
    eye = (row == col).astype(F32)
    gram[span:edge, :span] = side
    gram[:span, span:edge] = dot(eye, side, NT, HIGH)
    gram[span:edge, span:edge] = eye[:width, :width] * rows


def combine(weights, values):
    width = weights.shape[0]
    high, low = split(values)
    top, bottom = split(weights)
    first = dot(jnp.concatenate([top, bottom], 0), high, NN)
    return first[:width] + first[width:] + dot(top, low, NN)


def kernel(
    n_sta, n_cel, plane, height, cell_plane, depth, density, before, now, right_before,
    rights, left, alphas, betas,
    g_high, g_low, fs, turned, c_square, c_top, lhs, gp, forward, rhs, z_right, z_left,
    send_sta, send_cel, w_full, v_full, station_buf, cell_buf, small_right, small_share, small_left,
    gram_right, gram_left,
    sta_send, sta_recv, cel_send, cel_recv, sr_send, sr_recv, ss_send, ss_recv, sl_send, sl_recv,
):
    width, s_dev = now.shape
    c_dev = right_before.shape[1]
    places = {"sta": (lax.axis_index("sta"), n_sta), "cel": (lax.axis_index("cel"), n_cel)}
    cells = float(c_dev * n_cel)
    stations = float(s_dev * n_sta)

    def group(axis):
        me, n = places[axis]
        return [(o, lax.rem(me + o, n)) for o in range(1, n)]

    barrier = pltpu.get_barrier_semaphore()
    for axis in ("sta", "cel"):
        for _, peer in group(axis):
            pl.semaphore_signal(barrier, inc=1, device_id={axis: peer}, device_id_type=MESH)

    def send(axis, o, peer, source, target, sent, received):
        copy = pltpu.make_async_remote_copy(
            src_ref=source, dst_ref=target, send_sem=sent.at[o], recv_sem=received.at[o],
            device_id={axis: peer}, device_id_type=MESH)
        copy.start()
        return copy

    def finish(copies):
        for copy in copies:
            copy.wait()

    def columns(axis, index, extent):
        share = extent // places[axis][1]
        return pl.ds(pl.multiple_of(index * share, 128), share)

    def scatter(axis, step, source, buf, sent, received, produce, half_way):
        me, n = places[axis]
        copies, made, weights = [], [], None
        for position, (o, peer) in enumerate(group(axis) + [(0, me)]):
            span = columns(axis, peer, source.shape[1])
            if produce is not None:
                produce(span)
            made.append((o, peer, span))
            if position < n // 2 and half_way is not None:
                continue
            if weights is None and half_way is not None:
                weights = half_way()
            for o, peer, span in made:
                if weights is not None:
                    values, mixed = weights
                    source[:, span] = combine(mixed, values[:, span])
                if o:
                    copies.append(send(
                        axis, o, peer, source.at[:, span], buf.at[step, me],
                        sent.at[step, 0], received.at[step, 0]))
            made = []
        return copies

    def reduced(axis, step, copies, source, buf):
        me, n = places[axis]
        finish(copies)
        total = source[:, columns(axis, me, source.shape[1])]
        for o, peer in group(axis):
            total = total + buf[step, peer]
        return total

    def gather(axis, step, full, total, sent, received):
        span = columns(axis, places[axis][0], full.shape[2])
        full[step, :, span] = total
        block = full.at[step, :, span]
        return [
            send(axis, o, peer, block, block, sent.at[step, 1], received.at[step, 1])
            for o, peer in group(axis)
        ]

    def exchange(axis, step, values, buf, sent, received):
        me, n = places[axis]
        rows, cols = values.shape
        buf[step, me, :rows, :cols] = values
        block = buf.at[step, me, :rows]
        return [
            send(axis, o, peer, block, block, sent.at[step], received.at[step])
            for o, peer in group(axis)
        ]

    def collect(copies, step, rows, cols, buf):
        finish(copies)
        total = buf[step, 0, :rows, :cols]
        for index in range(1, buf.shape[1]):
            total = total + buf[step, index, :rows, :cols]
        return total

    def solve(step, sums, gram, count, lowers):
        span = sums.shape[1] - width
        if step == 0:
            gram[:span, :span] = sums[width:, width:]
        weights, lowers[step] = combination(sums[:width], gram[:span, :span], count)
        return weights

    station_features(fs, plane, height)
    cell_features(c_square, c_top, cell_plane, depth)
    high, low = split(now[...])
    lhs[:width], lhs[2 * width : 3 * width] = high, low
    high, low = split(before[...])
    lhs[width : 2 * width], lhs[3 * width :] = high, low
    row = lax.broadcasted_iota(jnp.int32, (FEATURES, FEATURES), 0)
    col = lax.broadcasted_iota(jnp.int32, (FEATURES, FEATURES), 1)
    eye = (row == col).astype(BF16)
    s_tile, c_tile, g_tile = min(1024, s_dev), 512, 256
    for start in range(0, s_dev, s_tile):
        rows = slice(start, start + s_tile)
        turned[rows, :] = dot(fs[:, rows].astype(BF16), eye, TN).astype(BF16)

    def make_columns(index, carry):
        cols = pl.ds(pl.multiple_of(index * g_tile, g_tile), g_tile)
        total = jnp.zeros((2 * width, g_tile), F32)
        c_low, c_high = c_square[:, cols].astype(BF16), c_top[:, cols].astype(BF16)
        for start in range(0, s_dev, s_tile):
            rows = slice(start, start + s_tile)
            square = dot(turned[rows, :], c_low, NN)
            top = dot(turned[rows, :], c_high, NN)
            inverse = lax.rsqrt(square)
            two = inverse * inverse
            high, low = split(two * two * (top * inverse))
            g_high[rows, cols] = high
            g_low[rows, cols] = low
            first = dot(lhs[:, rows], high, NN)
            total = total + (
                first[: 2 * width] + first[2 * width :] + dot(lhs[: 2 * width, rows], low, NN)
            )
        gp[: 2 * width, cols] = total
        return carry

    lax.fori_loop(0, c_dev // g_tile, make_columns, 0)
    send_sta[...] = gp[:width]
    gp[2 * width :] = gp[:width]
    pl.semaphore_wait(barrier, n_sta + n_cel - 2)
    copies = scatter("sta", 0, send_sta, station_buf, sta_send, sta_recv, None, None)

    c_me = places["cel"][0]
    for step in range(STEPS):
        last = step + 1 == STEPS
        total = reduced("sta", step, copies, send_sta, station_buf)
        total = total * (GAIN * density[:, columns("sta", places["sta"][0], c_dev)])
        finish(gather("sta", step, w_full, total, sta_send, sta_recv))
        w = w_full[step]
        z_right[:width] = w
        if step == 0:
            z_right[width : 2 * width] = right_before[...]
        r_rows = (step + 2) * width
        r_sent = width if step else r_rows
        small = exchange(
            "cel", step, products(z_right[:r_rows], r_sent), small_right, sr_send, sr_recv)
        gained = GAIN * density[...]
        high, low = split(w * gained)
        rhs[:width], rhs[2 * width : 3 * width] = high, low
        if step == 0:
            high, low = split(right_before[...] * gained)
            rhs[width : 2 * width], rhs[3 * width :] = high, low

        def forward_share(span):
            first = dot(rhs[...], g_high[span, :], NT)
            second = dot(rhs[: 2 * width], g_low[span, :], NT)
            both = first[: 2 * width] + first[2 * width :] + second
            if step == 0:
                forward[: 2 * width, span] = both
            else:
                forward[:width, span] = both[:width]

        right_sums = []

        def right_half_way():
            sums = collect(small, step, r_sent, r_rows, small_right)
            right_sums.append(sums)
            weights = solve(step, sums, gram_right, cells, alphas)
            right_sums.append(weights)
            return forward.at[:r_rows], weights

        copies = scatter(
            "cel", step, send_cel, cell_buf, cel_send, cel_recv, forward_share, right_half_way)
        sums, weights = right_sums
        right = combine(weights, z_right[:r_rows])
        rights[step] = right
        if not last:
            z_right[r_rows : r_rows + width] = right
            forward[r_rows : r_rows + width] = send_cel[...]
            grow(gram_right, weights, sums[:width, width:], cells)
        if step == 0:
            z_left[width : 2 * width] = before[...]
            z_left[2 * width : 3 * width] = now[...]

        total = reduced("cel", step, copies, send_cel, cell_buf)
        mine = columns("cel", c_me, s_dev)
        z_left[:width, mine] = total
        l_rows = (step + 3) * width
        l_sent = width if step else l_rows
        shared = exchange(
            "cel", step, products(z_left[:l_rows, mine], l_sent), small_share, ss_send, ss_recv)
        arriving = gather("cel", step, v_full, total, cel_send, cel_recv)

        def left_exchange():
            sums = collect(shared, step, l_sent, l_rows, small_share)
            return exchange("sta", step, sums, small_left, sl_send, sl_recv)

        if last:
            small = left_exchange()
            finish(arriving)
            z_left[:width] = v_full[step]
            sums = collect(small, step, l_sent, l_rows, small_left)
            left[...] = combine(solve(step, sums, gram_left, stations, betas), z_left[:l_rows])
            break

        def adjoint(rows, span):
            first = dot(lhs[: 2 * width, rows], g_high[rows, span], NN)
            return first[:width] + first[width:] + dot(lhs[:width, rows], g_low[rows, span], NN)

        def load(rows):
            high, low = split(v_full[step, :, rows])
            lhs[:width, rows], lhs[width : 2 * width, rows] = high, low

        load(mine)
        for start in range(0, c_dev, c_tile):
            span = slice(start, start + c_tile)
            gp[:width, span] = adjoint(mine, span)
        small = left_exchange()
        rows = mine
        for o, copy in enumerate(arriving, 1):
            copy.wait()
            rows = columns("cel", lax.rem(c_me + n_cel - o, n_cel), s_dev)
            load(rows)
            if o + 1 < n_cel:
                for start in range(0, c_dev, c_tile):
                    span = slice(start, start + c_tile)
                    gp[:width, span] += adjoint(rows, span)
        z_left[:width] = v_full[step]

        def adjoint_share(span):
            gp[:width, span] += adjoint(rows, span)

        left_sums = []

        def left_half_way():
            sums = collect(small, step, l_sent, l_rows, small_left)
            left_sums.append(sums)
            weights = solve(step, sums, gram_left, stations, betas)
            left_sums.append(weights)
            return gp.at[:l_rows], weights

        copies = scatter(
            "sta", step + 1, send_sta, station_buf, sta_send, sta_recv, adjoint_share, left_half_way)
        sums, weights = left_sums
        z_left[l_rows : l_rows + width] = combine(weights, z_left[:l_rows])
        grow(gram_left, weights, sums[:width, width:], stations)
        if step + 2 < STEPS:
            gp[l_rows : l_rows + width] = send_sta[...]


def body(plane, height, cell_plane, depth, density, before, now, right_before):
    width, s_dev = now.shape
    c_dev = right_before.shape[1]
    n_sta = lax.axis_size("sta")
    n_cel = lax.axis_size("cel")
    vmem = pl.BlockSpec(memory_space=pltpu.VMEM)
    dma = pltpu.SemaphoreType.DMA
    lanes = 128
    out_shape = (
        jax.ShapeDtypeStruct((STEPS, width, c_dev), F32),
        jax.ShapeDtypeStruct((width, s_dev), F32),
        jax.ShapeDtypeStruct((STEPS, width, width), F32),
        jax.ShapeDtypeStruct((STEPS, width, width), F32),
    )
    scratch = [
        pltpu.VMEM((s_dev, c_dev), BF16),
        pltpu.VMEM((s_dev, c_dev), BF16),
        pltpu.VMEM((FEATURES, s_dev), F32),
        pltpu.VMEM((s_dev, FEATURES), BF16),
        pltpu.VMEM((FEATURES, c_dev), F32),
        pltpu.VMEM((FEATURES, c_dev), F32),
        pltpu.VMEM((4 * width, s_dev), BF16),
        pltpu.VMEM(((STEPS + 1) * width, c_dev), F32),
        pltpu.VMEM(((STEPS + 1) * width, s_dev), F32),
        pltpu.VMEM((4 * width, c_dev), BF16),
        pltpu.VMEM(((STEPS + 1) * width, c_dev), F32),
        pltpu.VMEM(((STEPS + 2) * width, s_dev), F32),
        pltpu.VMEM((width, c_dev), F32),
        pltpu.VMEM((width, s_dev), F32),
        pltpu.VMEM((STEPS, width, c_dev), F32),
        pltpu.VMEM((STEPS, width, s_dev), F32),
        pltpu.VMEM((STEPS, n_sta, width, c_dev // n_sta), F32),
        pltpu.VMEM((STEPS, n_cel, width, s_dev // n_cel), F32),
        pltpu.VMEM((STEPS, n_cel, (STEPS + 1) * width, lanes), F32),
        pltpu.VMEM((STEPS, n_cel, (STEPS + 2) * width, lanes), F32),
        pltpu.VMEM((STEPS, n_sta, (STEPS + 2) * width, lanes), F32),
        pltpu.VMEM(((STEPS + 1) * width, lanes), F32),
        pltpu.VMEM(((STEPS + 2) * width, lanes), F32),
        dma((STEPS, 2, n_sta)),
        dma((STEPS, 2, n_sta)),
        dma((STEPS, 2, n_cel)),
        dma((STEPS, 2, n_cel)),
        dma((STEPS, n_cel)),
        dma((STEPS, n_cel)),
        dma((STEPS, n_cel)),
        dma((STEPS, n_cel)),
        dma((STEPS, n_sta)),
        dma((STEPS, n_sta)),
    ]
    return pl.pallas_call(
        functools.partial(kernel, n_sta, n_cel),
        out_shape=out_shape,
        in_specs=[vmem] * 8,
        out_specs=(vmem,) * 4,
        scratch_shapes=scratch,
        compiler_params=pltpu.CompilerParams(
            collective_id=0, has_side_effects=True, vmem_limit_bytes=56 * 1024 * 1024
        ),
        cost_estimate=pl.CostEstimate(
            flops=2 * 3 * 2 * STEPS * width * s_dev * c_dev, bytes_accessed=4 * 1024 * 1024, transcendentals=s_dev * c_dev
        ),
    )(plane, height[None, :], cell_plane, depth[None, :], density[None, :], before, now, right_before)


def solution(mesh):
    in_specs = (
        P(None, "sta"),
        P("sta"),
        P(None, "cel"),
        P("cel"),
        P("cel"),
        P(None, "sta"),
        P(None, "sta"),
        P(None, "cel"),
    )
    out_specs = (P(None, None, "cel"), P(None, "sta"), P(), P())
    return jax.shard_map(body, mesh=mesh, in_specs=in_specs, out_specs=out_specs, check_vma=False)
```

```python
import functools

import jax
import jax.numpy as jnp
from jax import lax
from jax.experimental import pallas as pl
from jax.experimental.pallas import tpu as pltpu
from jax.sharding import PartitionSpec as P

STEPS = 2
GAIN = 4.0
CENTER = 96.0
FEATURES = 16
HIGH = lax.Precision.HIGHEST
F32 = jnp.float32
BF16 = jnp.bfloat16
MESH = pl.DeviceIdType.MESH
NN = (((1,), (0,)), ((), ()))
NT = (((1,), (1,)), ((), ()))
TN = (((0,), (0,)), ((), ()))


def dot(a, b, dims, precision=None):
    return lax.dot_general(a, b, dims, precision=precision, preferred_element_type=F32)


def split(values):
    high = values.astype(BF16)
    return high, (values - high.astype(F32)).astype(BF16)


def fill_features(ref, rows):
    for index, row in enumerate(rows):
        ref[index : index + 1, :] = row
    ref[len(rows) :, :] = jnp.zeros((FEATURES - len(rows), ref.shape[1]), F32)


def coordinates(plane, level):
    x = plane[0:1, :].astype(F32) - CENTER
    y = plane[1:2, :].astype(F32) - CENTER
    z = level[...].astype(F32)
    flat = x * x + y * y
    high = jnp.floor(flat / 256.0) * 256.0
    return x, y, z, high, flat - high, jnp.ones_like(x)


def station_features(ref, plane, height):
    x, y, z, high, low, one = coordinates(plane, height)
    fill_features(ref, [high, low, one, one, x, y, z * z, z, one, one])


def cell_features(square, top, plane, depth):
    x, y, z, high, low, one = coordinates(plane, depth)
    inner = z * z + z
    rows = [one, one, high, low, -2.0 * x, -2.0 * y, one, 2.0 * z + one, inner, 0.25 * one]
    fill_features(square, rows)
    rows = [-one, -one, -high, -low, 2.0 * x, 2.0 * y, 2.0 * one, 4.0 * z + 2.0 * one]
    fill_features(top, rows + [2.0 * inner, 0.5 * one])


def eliminate(gram):
    width = gram.shape[0]
    row = lax.broadcasted_iota(jnp.int32, (width, width), 0)
    col = lax.broadcasted_iota(jnp.int32, (width, width), 1)
    eye = (row == col).astype(F32)
    upper, inverse = gram, eye
    for j in range(width - 1):
        pivot = upper[j : j + 1, :]
        factor = jnp.where(row[:, :1] > j, upper[:, j : j + 1] / pivot[:, j : j + 1], 0.0)
        upper = upper - factor * pivot
        inverse = inverse - factor * inverse[j : j + 1, :]
    scale = lax.rsqrt(jnp.sum(eye * upper, axis=1, keepdims=True))
    upper = jnp.where(col >= row, upper * scale, 0.0)
    lower = dot(upper, eye, TN, HIGH)
    return inverse * scale, lower


def combination(sums, basis_gram, rows):
    width, total = sums.shape
    scaled = sums / rows
    square, coef = scaled[:, :width], scaled[:, width:]
    span = total - width
    twice = (
        lax.broadcasted_iota(jnp.int32, (span, span), 0)
        == lax.broadcasted_iota(jnp.int32, (span, span), 1)
    )
    inner = jnp.where(twice, 2.0, 0.0) - basis_gram / rows
    gram = square - dot(dot(coef, inner, NN, HIGH), coef, NT, HIGH)
    inverse, lower = eliminate(gram)
    row = lax.broadcasted_iota(jnp.int32, (width, total), 0)
    col = lax.broadcasted_iota(jnp.int32, (width, total), 1)
    weights = dot(inverse, jnp.where(col < width, (row == col).astype(F32), -scaled), NN, HIGH)
    return weights, lower


def products(values, count):
    high, low = split(values)
    return dot(high[:count], high, NT) + dot(high[:count], low, NT) + dot(low[:count], high, NT)


def grow(gram, weights, cross, rows):
    width, span = cross.shape
    basis = gram[:span, :span]
    side = dot(weights[:, :width], cross, NN, HIGH) + dot(weights[:, width:], basis, NN, HIGH)
    edge = span + width
    row = lax.broadcasted_iota(jnp.int32, (span, span), 0)
    col = lax.broadcasted_iota(jnp.int32, (span, span), 1)
    eye = (row == col).astype(F32)
    gram[span:edge, :span] = side
    gram[:span, span:edge] = dot(eye, side, NT, HIGH)
    gram[span:edge, span:edge] = eye[:width, :width] * rows


def combine(weights, values):
    width = weights.shape[0]
    high, low = split(values)
    top, bottom = split(weights)
    first = dot(jnp.concatenate([top, bottom], 0), high, NN)
    return first[:width] + first[width:] + dot(top, low, NN)


def kernel(
    n_sta, n_cel, plane, height, cell_plane, depth, density, before, now, right_before,
    rights, left, alphas, betas,
    g_high, g_low, fs, turned, c_square, c_top, lhs, gp, forward, rhs, rhs_low, z_right, z_left,
    send_sta, send_cel, w_full, v_full, station_buf, cell_buf, small_right, small_share, small_left,
    gram_right, gram_left,
    sta_send, sta_recv, cel_send, cel_recv, sr_send, sr_recv, ss_send, ss_recv, sl_send, sl_recv,
):
    width, s_dev = now.shape
    c_dev = right_before.shape[1]
    places = {"sta": (lax.axis_index("sta"), n_sta), "cel": (lax.axis_index("cel"), n_cel)}
    cells = float(c_dev * n_cel)
    stations = float(s_dev * n_sta)

    def group(axis):
        me, n = places[axis]
        return [(o, lax.rem(me + o, n)) for o in range(1, n)]

    barrier = pltpu.get_barrier_semaphore()
    for axis in ("sta", "cel"):
        for _, peer in group(axis):
            pl.semaphore_signal(barrier, inc=1, device_id={axis: peer}, device_id_type=MESH)

    def send(axis, o, peer, source, target, sent, received):
        copy = pltpu.make_async_remote_copy(
            src_ref=source, dst_ref=target, send_sem=sent.at[o], recv_sem=received.at[o],
            device_id={axis: peer}, device_id_type=MESH)
        copy.start()
        return copy

    def finish(copies):
        for copy in copies:
            copy.wait()

    def columns(axis, index, extent):
        share = extent // places[axis][1]
        return pl.ds(pl.multiple_of(index * share, 128), share)

    def scatter(axis, step, source, buf, sent, received, produce, half_way):
        me, n = places[axis]
        copies, made, weights = [], [], None
        for position, (o, peer) in enumerate(group(axis) + [(0, me)]):
            span = columns(axis, peer, source.shape[1])
            if produce is not None:
                produce(span)
            made.append((o, peer, span))
            if position < n // 2 and half_way is not None:
                continue
            if weights is None and half_way is not None:
                weights = half_way()
            for o, peer, span in made:
                if weights is not None:
                    values, mixed = weights
                    source[:, span] = combine(mixed, values[:, span])
                if o:
                    copies.append(send(
                        axis, o, peer, source.at[:, span], buf.at[step, me],
                        sent.at[step, 0], received.at[step, 0]))
            made = []
        return copies

    def reduced(axis, step, copies, source, buf):
        me, n = places[axis]
        finish(copies)
        total = source[:, columns(axis, me, source.shape[1])]
        for o, peer in group(axis):
            total = total + buf[step, peer]
        return total

    def gather(axis, step, full, total, sent, received):
        span = columns(axis, places[axis][0], full.shape[2])
        full[step, :, span] = total
        block = full.at[step, :, span]
        return [
            send(axis, o, peer, block, block, sent.at[step, 1], received.at[step, 1])
            for o, peer in group(axis)
        ]

    def exchange(axis, step, values, buf, sent, received):
        me, n = places[axis]
        rows, cols = values.shape
        buf[step, me, :rows, :cols] = values
        block = buf.at[step, me, :rows]
        return [
            send(axis, o, peer, block, block, sent.at[step], received.at[step])
            for o, peer in group(axis)
        ]

    def collect(copies, step, rows, cols, buf):
        finish(copies)
        total = buf[step, 0, :rows, :cols]
        for index in range(1, buf.shape[1]):
            total = total + buf[step, index, :rows, :cols]
        return total

    def solve(step, sums, gram, count, lowers):
        span = sums.shape[1] - width
        if step == 0:
            gram[:span, :span] = sums[width:, width:]
        weights, lowers[step] = combination(sums[:width], gram[:span, :span], count)
        return weights

    station_features(fs, plane, height)
    cell_features(c_square, c_top, cell_plane, depth)
    high, low = split(now[...])
    lhs[:width], lhs[2 * width : 3 * width] = high, low
    high, low = split(before[...])
    lhs[width : 2 * width], lhs[3 * width :] = high, low
    row = lax.broadcasted_iota(jnp.int32, (FEATURES, FEATURES), 0)
    col = lax.broadcasted_iota(jnp.int32, (FEATURES, FEATURES), 1)
    eye = (row == col).astype(BF16)
    s_tile, c_tile, g_tile = min(1024, s_dev), 512, 256
    for start in range(0, s_dev, s_tile):
        rows = slice(start, start + s_tile)
        turned[rows, :] = dot(fs[:, rows].astype(BF16), eye, TN).astype(BF16)

    def make_columns(index, carry):
        cols = pl.ds(pl.multiple_of(index * g_tile, g_tile), g_tile)
        total = jnp.zeros((2 * width, g_tile), F32)
        c_low, c_high = c_square[:, cols].astype(BF16), c_top[:, cols].astype(BF16)
        for start in range(0, s_dev, s_tile):
            rows = slice(start, start + s_tile)
            square = dot(turned[rows, :], c_low, NN)
            top = dot(turned[rows, :], c_high, NN)
            inverse = lax.rsqrt(square)
            two = inverse * inverse
            high, low = split(two * two * (top * inverse))
            g_high[rows, cols] = high
            g_low[rows, cols] = low
            first = dot(lhs[:, rows], high, NN)
            total = total + (
                first[: 2 * width] + first[2 * width :] + dot(lhs[: 2 * width, rows], low, NN)
            )
        gp[: 2 * width, cols] = total
        return carry

    lax.fori_loop(0, c_dev // g_tile, make_columns, 0)
    send_sta[...] = gp[:width]
    gp[2 * width :] = gp[:width]
    pl.semaphore_wait(barrier, n_sta + n_cel - 2)
    copies = scatter("sta", 0, send_sta, station_buf, sta_send, sta_recv, None, None)

    c_me = places["cel"][0]
    for step in range(STEPS):
        last = step + 1 == STEPS
        total = reduced("sta", step, copies, send_sta, station_buf)
        total = total * (GAIN * density[:, columns("sta", places["sta"][0], c_dev)])
        finish(gather("sta", step, w_full, total, sta_send, sta_recv))
        w = w_full[step]
        z_right[:width] = w
        if step == 0:
            z_right[width : 2 * width] = right_before[...]
        r_rows = (step + 2) * width
        r_sent = width if step else r_rows
        small = exchange(
            "cel", step, products(z_right[:r_rows], r_sent), small_right, sr_send, sr_recv)
        gained = GAIN * density[...]
        high, low = split(w * gained)
        rhs[:width], rhs[2 * width : 3 * width] = high, low
        if step == 0:
            high, low = split(right_before[...] * gained)
            rhs[width : 2 * width], rhs[3 * width : 4 * width] = high, low
            rhs[4 * width :] = jnp.zeros((rhs.shape[0] - 4 * width, c_dev), BF16)
            rhs_low[2 * width :] = jnp.zeros((rhs.shape[0] - 2 * width, c_dev), BF16)
        rhs_low[: 2 * width] = rhs[: 2 * width]

        def forward_share(span):
            first = dot(g_high[span, :], rhs[...], NT) + dot(g_low[span, :], rhs_low[...], NT)
            first = first.T
            both = first[: 2 * width] + first[2 * width : 4 * width]
            if step == 0:
                forward[: 2 * width, span] = both
            else:
                forward[:width, span] = both[:width]

        right_sums = []

        def right_half_way():
            sums = collect(small, step, r_sent, r_rows, small_right)
            right_sums.append(sums)
            weights = solve(step, sums, gram_right, cells, alphas)
            right_sums.append(weights)
            return forward.at[:r_rows], weights

        copies = scatter(
            "cel", step, send_cel, cell_buf, cel_send, cel_recv, forward_share, right_half_way)
        sums, weights = right_sums
        right = combine(weights, z_right[:r_rows])
        rights[step] = right
        if not last:
            z_right[r_rows : r_rows + width] = right
            forward[r_rows : r_rows + width] = send_cel[...]
            grow(gram_right, weights, sums[:width, width:], cells)
        if step == 0:
            z_left[width : 2 * width] = before[...]
            z_left[2 * width : 3 * width] = now[...]

        total = reduced("cel", step, copies, send_cel, cell_buf)
        mine = columns("cel", c_me, s_dev)
        z_left[:width, mine] = total
        l_rows = (step + 3) * width
        l_sent = width if step else l_rows
        shared = exchange(
            "cel", step, products(z_left[:l_rows, mine], l_sent), small_share, ss_send, ss_recv)
        arriving = gather("cel", step, v_full, total, cel_send, cel_recv)

        def left_exchange():
            sums = collect(shared, step, l_sent, l_rows, small_share)
            return exchange("sta", step, sums, small_left, sl_send, sl_recv)

        if last:
            small = left_exchange()
            finish(arriving)
            z_left[:width] = v_full[step]
            sums = collect(small, step, l_sent, l_rows, small_left)
            left[...] = combine(solve(step, sums, gram_left, stations, betas), z_left[:l_rows])
            break

        def adjoint(rows, span):
            first = dot(lhs[: 2 * width, rows], g_high[rows, span], NN)
            return first[:width] + first[width:] + dot(lhs[:width, rows], g_low[rows, span], NN)

        def load(rows):
            high, low = split(v_full[step, :, rows])
            lhs[:width, rows], lhs[width : 2 * width, rows] = high, low

        load(mine)
        for start in range(0, c_dev, c_tile):
            span = slice(start, start + c_tile)
            gp[:width, span] = adjoint(mine, span)
        small = left_exchange()
        rows = mine
        for o, copy in enumerate(arriving, 1):
            copy.wait()
            rows = columns("cel", lax.rem(c_me + n_cel - o, n_cel), s_dev)
            load(rows)
            if o + 1 < n_cel:
                for start in range(0, c_dev, c_tile):
                    span = slice(start, start + c_tile)
                    gp[:width, span] += adjoint(rows, span)
        z_left[:width] = v_full[step]

        def adjoint_share(span):
            gp[:width, span] += adjoint(rows, span)

        left_sums = []

        def left_half_way():
            sums = collect(small, step, l_sent, l_rows, small_left)
            left_sums.append(sums)
            weights = solve(step, sums, gram_left, stations, betas)
            left_sums.append(weights)
            return gp.at[:l_rows], weights

        copies = scatter(
            "sta", step + 1, send_sta, station_buf, sta_send, sta_recv, adjoint_share, left_half_way)
        sums, weights = left_sums
        z_left[l_rows : l_rows + width] = combine(weights, z_left[:l_rows])
        grow(gram_left, weights, sums[:width, width:], stations)
        if step + 2 < STEPS:
            gp[l_rows : l_rows + width] = send_sta[...]


def body(plane, height, cell_plane, depth, density, before, now, right_before):
    width, s_dev = now.shape
    c_dev = right_before.shape[1]
    n_sta = lax.axis_size("sta")
    n_cel = lax.axis_size("cel")
    vmem = pl.BlockSpec(memory_space=pltpu.VMEM)
    dma = pltpu.SemaphoreType.DMA
    lanes = 128
    out_shape = (
        jax.ShapeDtypeStruct((STEPS, width, c_dev), F32),
        jax.ShapeDtypeStruct((width, s_dev), F32),
        jax.ShapeDtypeStruct((STEPS, width, width), F32),
        jax.ShapeDtypeStruct((STEPS, width, width), F32),
    )
    scratch = [
        pltpu.VMEM((s_dev, c_dev), BF16),
        pltpu.VMEM((s_dev, c_dev), BF16),
        pltpu.VMEM((FEATURES, s_dev), F32),
        pltpu.VMEM((s_dev, FEATURES), BF16),
        pltpu.VMEM((FEATURES, c_dev), F32),
        pltpu.VMEM((FEATURES, c_dev), F32),
        pltpu.VMEM((4 * width, s_dev), BF16),
        pltpu.VMEM(((STEPS + 1) * width, c_dev), F32),
        pltpu.VMEM(((STEPS + 1) * width, s_dev), F32),
        pltpu.VMEM((lanes, c_dev), BF16),
        pltpu.VMEM((lanes, c_dev), BF16),
        pltpu.VMEM(((STEPS + 1) * width, c_dev), F32),
        pltpu.VMEM(((STEPS + 2) * width, s_dev), F32),
        pltpu.VMEM((width, c_dev), F32),
        pltpu.VMEM((width, s_dev), F32),
        pltpu.VMEM((STEPS, width, c_dev), F32),
        pltpu.VMEM((STEPS, width, s_dev), F32),
        pltpu.VMEM((STEPS, n_sta, width, c_dev // n_sta), F32),
        pltpu.VMEM((STEPS, n_cel, width, s_dev // n_cel), F32),
        pltpu.VMEM((STEPS, n_cel, (STEPS + 1) * width, lanes), F32),
        pltpu.VMEM((STEPS, n_cel, (STEPS + 2) * width, lanes), F32),
        pltpu.VMEM((STEPS, n_sta, (STEPS + 2) * width, lanes), F32),
        pltpu.VMEM(((STEPS + 1) * width, lanes), F32),
        pltpu.VMEM(((STEPS + 2) * width, lanes), F32),
        dma((STEPS, 2, n_sta)),
        dma((STEPS, 2, n_sta)),
        dma((STEPS, 2, n_cel)),
        dma((STEPS, 2, n_cel)),
        dma((STEPS, n_cel)),
        dma((STEPS, n_cel)),
        dma((STEPS, n_cel)),
        dma((STEPS, n_cel)),
        dma((STEPS, n_sta)),
        dma((STEPS, n_sta)),
    ]
    return pl.pallas_call(
        functools.partial(kernel, n_sta, n_cel),
        out_shape=out_shape,
        in_specs=[vmem] * 8,
        out_specs=(vmem,) * 4,
        scratch_shapes=scratch,
        compiler_params=pltpu.CompilerParams(
            collective_id=0, has_side_effects=True, vmem_limit_bytes=56 * 1024 * 1024
        ),
        cost_estimate=pl.CostEstimate(
            flops=2 * 3 * 2 * STEPS * width * s_dev * c_dev, bytes_accessed=4 * 1024 * 1024, transcendentals=s_dev * c_dev
        ),
    )(plane, height[None, :], cell_plane, depth[None, :], density[None, :], before, now, right_before)


def solution(mesh):
    in_specs = (
        P(None, "sta"),
        P("sta"),
        P(None, "cel"),
        P("cel"),
        P("cel"),
        P(None, "sta"),
        P(None, "sta"),
        P(None, "cel"),
    )
    out_specs = (P(None, None, "cel"), P(None, "sta"), P(), P())
    return jax.shard_map(body, mesh=mesh, in_specs=in_specs, out_specs=out_specs, check_vma=False)
```
